512 devices in a mesh: seq: 32 (over x, z), mp: 16 (over y, core).
Axes of the slice: x: 4, y: 8, z: 8, core: 2. Of those that a mesh axis runs over, the one named last changes fastest.
Arguments:
- inputs: bfloat16 [8192, 16384], P('seq', 'mp'), may hold values from -6 to 6
- conv_weight: float32 [4, 16384], P(None, 'mp'), may hold values from -3 to 3
- conv_bias: float32 [16384], P('mp'), may hold values from -3 to 3
- proj_weight: bfloat16 [16384, 544], P('mp'), may hold values from -0.046875 to 0.046875
- dt_weight: bfloat16 [512, 16384], P(None, 'mp'), may hold values from -0.25 to 0.25
- dt_bias: float32 [16384], P('mp'), may hold values from -6.9 to -2.3
- decay_rate: float32 [16384, 16], P('mp'), may hold values from 0.01 to 10
- skip_gain: float32 [16384], P('mp'), may hold values from 0.5 to 1.5
Outputs:
- scanned: bfloat16 [8192, 16384], P('seq', 'mp')
The draws below stay inside these ranges and needn't reach their ends.
All inputs are finite; a program needn't handle non-finite values.
Results may differ from the reference program's by a relative error of at most 0.014.
Values may be sent and summed in bfloat16 or wider, within the bound.
No kernel may reach another device: no remote copies, remote signals or barrier semaphores. Data moves between devices by JAX's collectives and lax.ppermute only.
A program may use at most 64 MiB of HBM per device.

```python
import math
import jax
import jax.numpy as jnp
from jax import lax

CHANNELS = 16384
STATE = 16
DT_RANK = 512
KERNEL = 4
TOKENS = 8192


def block_levels(key, shape, cuts, low, largest):
    def one(axis_at, blocks):
        heights = jax.random.uniform(jax.random.fold_in(jax.random.fold_in(key, 6), axis_at), (blocks,), jnp.float32, low / len(cuts), largest / len(cuts))
        return jnp.repeat(jnp.exp(heights), shape[axis_at] // blocks).reshape((-1,) + (1,) * (len(shape) - axis_at - 1))

    factor_of = one(*cuts[0])
    for cut in cuts[1:]:
        factor_of = factor_of * one(*cut)
    return factor_of


def normal_values(rng, extent, deviation, bound, split=(), kind=jnp.bfloat16):
    loudness = block_levels(rng, extent, split, -0.22, 0.18) if split else 1.0
    entries = jax.random.normal(rng, extent, jnp.float32) * deviation * loudness
    return jnp.minimum(jnp.maximum(entries, -bound), bound).astype(kind)


def setup_inputs(seed: int = 0) -> dict:
    arg_keys = jax.random.split(jax.random.key(seed), 9)
    inputs = normal_values(arg_keys[0], (TOKENS, CHANNELS), 1.0, 6.0, ((0, 32), (1, 16)))
    conv_weight = normal_values(arg_keys[1], (KERNEL, CHANNELS), KERNEL ** -0.5, 3.0, ((1, 16),), jnp.float32)
    conv_bias = normal_values(arg_keys[2], (CHANNELS,), 0.5, 3.0, ((0, 16),), jnp.float32)
    proj_weight = normal_values(arg_keys[3], (CHANNELS, DT_RANK + 2 * STATE), CHANNELS ** -0.5, 0.046875, ((0, 16),))
    dt_weight = normal_values(arg_keys[4], (DT_RANK, CHANNELS), DT_RANK ** -0.5, 0.25, ((1, 16),))
    dt_bias = jnp.clip(-6.9 + 4.6000001430511475 * jax.random.uniform(arg_keys[5], (CHANNELS,), jnp.float32) ** block_levels(arg_keys[5], (CHANNELS,), ((0, 16),), -0.2, 0.2), -6.9, -2.3)
    decay_rate = jnp.clip(jnp.exp(math.log(10.0) - 6.9077553 * jax.random.uniform(arg_keys[6], (CHANNELS, STATE), jnp.float32) ** block_levels(arg_keys[6], (CHANNELS, STATE), ((0, 16),), -0.2, 0.2)), 0.01, 10.0)
    skip_gain = jnp.clip(0.5 + 1.0 * jax.random.uniform(arg_keys[7], (CHANNELS,), jnp.float32) ** block_levels(arg_keys[7], (CHANNELS,), ((0, 16),), -0.2, 0.2), 0.5, 1.5)
    return dict(inputs=inputs, conv_weight=conv_weight, conv_bias=conv_bias, proj_weight=proj_weight, dt_weight=dt_weight, dt_bias=dt_bias, decay_rate=decay_rate, skip_gain=skip_gain)


def reference(inputs, conv_weight, conv_bias, proj_weight, dt_weight, dt_bias, decay_rate, skip_gain):
    length = inputs.shape[0]
    groups = 16
    width = inputs.shape[1] // groups
    padded = jnp.concatenate([jnp.zeros((3, inputs.shape[1]), inputs.dtype), inputs], axis=0)

    def convolve(total, index):
        start = (index * width).astype(jnp.int32)
        rows = lax.dynamic_slice_in_dim(padded, start, width, 1).astype(jnp.float32)
        taps = lax.dynamic_slice_in_dim(conv_weight, start, width, 1)
        bias = lax.dynamic_slice_in_dim(conv_bias, start, width, 0)
        pre = bias + taps[0] * rows[0:length] + taps[1] * rows[1:length + 1]
        pre = pre + taps[2] * rows[2:length + 2] + taps[3] * rows[3:length + 3]
        mixed = jax.nn.silu(pre).astype(jnp.bfloat16)
        weights = lax.dynamic_slice_in_dim(proj_weight, start, width, 0)
        return total + jnp.dot(mixed, weights, preferred_element_type=jnp.float32), mixed

    start_total = jnp.zeros((length, proj_weight.shape[1]), jnp.float32)
    projected, mixed_all = lax.scan(convolve, start_total, jnp.arange(groups, dtype=jnp.int32))
    low = projected[:, :DT_RANK].astype(jnp.bfloat16)
    entry = projected[:, DT_RANK:DT_RANK + STATE]
    readout = projected[:, DT_RANK + STATE:]

    def scan_group(index):
        start = (index * width).astype(jnp.int32)
        values = mixed_all[index].astype(jnp.float32)
        weights = lax.dynamic_slice_in_dim(dt_weight, start, width, 1)
        bias = lax.dynamic_slice_in_dim(dt_bias, start, width, 0)
        steps_dt = jax.nn.softplus(jnp.dot(low, weights, preferred_element_type=jnp.float32) + bias)
        rates = -lax.dynamic_slice_in_dim(decay_rate, start, width, 0)
        gains = lax.dynamic_slice_in_dim(skip_gain, start, width, 0)

        def step(state, row):
            delta, value, enter, read = row
            state = jnp.exp(delta[:, None] * rates) * state + (delta * value)[:, None] * enter[None, :]
            return state, jnp.sum(state * read[None, :], axis=1)

        _, outputs = lax.scan(step, jnp.zeros((width, STATE), jnp.float32), (steps_dt, values, entry, readout))
        return (outputs + gains * values).astype(jnp.bfloat16)

    results = lax.map(scan_group, jnp.arange(groups, dtype=jnp.int32))
    return jnp.transpose(results, (1, 0, 2)).reshape(length, groups * width)
```

```python
import jax
import jax.numpy as jnp
from jax import lax
from jax.experimental import pallas as pl
from jax.experimental.pallas import tpu as pltpu
from jax.sharding import PartitionSpec as P

F32, BF16 = jnp.float32, jnp.bfloat16
STATE = 16
DT_RANK = 512
LANES = 128
LOG2E = 1.4426950408889634
VMEM = pl.BlockSpec(memory_space=pltpu.VMEM)
PARAMS = pltpu.CompilerParams(vmem_limit_bytes=32 << 20)


def front_kernel(x_ref, halo_ref, w_ref, b_ref, pw_ref, mixed_ref, part_ref, pad_ref):
    rows = x_ref.shape[0]
    pad_ref[0:8, :] = halo_ref[...].astype(F32)
    step = 16
    for r in range(0, rows, step):
        pad_ref[8 + r : 8 + r + step, :] = x_ref[r : r + step, :].astype(F32)
        pre = b_ref[...] + w_ref[0:1, :] * pad_ref[r + 5 : r + 5 + step, :]
        for k in range(1, 4):
            pre = pre + w_ref[k : k + 1, :] * pad_ref[r + 5 + k : r + 5 + k + step, :]
        mixed_ref[r : r + step, :] = (pre / (1.0 + jnp.exp(-pre))).astype(BF16)
    part_ref[...] = lax.dot_general(
        mixed_ref[...], pw_ref[...], (((1,), (1,)), ((), ())), preferred_element_type=F32
    ).astype(BF16)


def front(x, halo, taps, bias, weight_t):
    rows, width = x.shape
    return pl.pallas_call(
        front_kernel,
        out_shape=(
            jax.ShapeDtypeStruct((rows, width), BF16),
            jax.ShapeDtypeStruct((rows, weight_t.shape[0]), BF16),
        ),
        in_specs=[VMEM] * 5,
        out_specs=(VMEM, VMEM),
        scratch_shapes=[pltpu.VMEM((rows + 8, width), F32)],
        compiler_params=PARAMS,
        name="front",
    )(x, halo, taps, bias, weight_t)


def spread(columns, first, count, out_ref):
    for n in range(count):
        out_ref[n] = jnp.broadcast_to(
            columns[:, first + n : first + n + 1], (columns.shape[0], LANES)
        )


def fold_rates(decay_ref, rate_ref):
    tiles = decay_ref.shape[1] // LANES
    for j in range(tiles):
        rate_ref[pl.ds(j, STATE, tiles), :] = decay_ref[:, LANES * j : LANES * (j + 1)] * -LOG2E


def scan_kernel(
    g_ref, dtw_ref, dtb_ref, mixed_ref, decay_ref, y_ref, cum_ref, send_ref,
    dt_ref, dx_ref, bc_ref, rate_ref,
):
    rows, width = mixed_ref.shape
    tiles = width // LANES
    fold_rates(decay_ref, rate_ref)
    low = g_ref[:, 0:DT_RANK]
    for c in range(0, width, 256):
        pre = jnp.dot(low, dtw_ref[:, c : c + 256], preferred_element_type=F32)
        pre = pre + dtb_ref[:, c : c + 256]
        dt = jnp.maximum(pre, 0.0) + jnp.log1p(jnp.exp(-jnp.abs(pre)))
        dx = dt * mixed_ref[:, c : c + 256].astype(F32)
        for h in range(2):
            at = pl.ds(c // LANES + h, rows, tiles)
            dt_ref[at, :] = dt[:, LANES * h : LANES * (h + 1)]
            dx_ref[at, :] = dx[:, LANES * h : LANES * (h + 1)]
    spread(g_ref[:, DT_RANK : DT_RANK + 2 * STATE].astype(F32), 0, 2 * STATE, bc_ref)
    unroll = 8

    def rate(n):
        return rate_ref[tiles * n : tiles * (n + 1), :]

    def group(i, carry):
        states, total = list(carry[:STATE]), carry[STATE]
        t0 = pl.multiple_of(i * unroll, unroll)
        for r in range(unroll):
            at = pl.ds(pl.multiple_of((t0 + r) * tiles, tiles), tiles)
            dt, dx = dt_ref[at, :], dx_ref[at, :]
            total = total + dt
            cum_ref[at, :] = total
            y = jnp.zeros_like(dt)
            for n in range(STATE):
                enter = jnp.broadcast_to(bc_ref[n, pl.ds(t0 + r, 1), :], dt.shape)
                read = jnp.broadcast_to(bc_ref[STATE + n, pl.ds(t0 + r, 1), :], dt.shape)
                states[n] = jnp.exp2(dt * rate(n)) * states[n] + dx * enter
                y = y + states[n] * read
            y_ref[at, :] = y
        return (*states, total)

    zero = jnp.zeros((tiles, LANES), F32)
    final = lax.fori_loop(0, rows // unroll, group, (zero,) * (STATE + 1))
    half = tiles // 2
    for n in range(STATE):
        state, lost = final[n], 1.0 - jnp.exp2(final[STATE] * rate(n))
        pieces = [state[:half], lost[:half], state[half:], lost[half:]]
        send_ref[2 * tiles * n : 2 * tiles * (n + 1), :] = jnp.concatenate(pieces, axis=0).astype(BF16)


def scan(g, dtw, dtb, mixed, decay):
    rows, width = mixed.shape
    tiles = width // LANES
    flat = jax.ShapeDtypeStruct((rows * tiles, LANES), F32)
    return pl.pallas_call(
        scan_kernel,
        out_shape=(flat, flat, jax.ShapeDtypeStruct((2 * STATE * tiles, LANES), BF16)),
        in_specs=[VMEM] * 5,
        out_specs=(VMEM,) * 3,
        scratch_shapes=[
            pltpu.VMEM(flat.shape, F32),
            pltpu.VMEM(flat.shape, F32),
            pltpu.VMEM((2 * STATE, rows, LANES), F32),
            pltpu.VMEM((STATE * tiles, LANES), F32),
        ],
        compiler_params=PARAMS,
        name="scan",
    )(g, dtw, dtb, mixed, decay)


def prefix_kernel(got_ref, out_ref):
    blocks = got_ref.shape[0] // 8
    half = 4
    state = jnp.zeros((half, LANES), F32)
    for pair in range(blocks // 2):
        block = got_ref[16 * pair : 16 * (pair + 1), :].astype(F32)
        held = []
        for h in range(2):
            held.append(state)
            end, lost = block[8 * h : 8 * h + half], block[8 * h + half : 8 * h + 8]
            state = state - lost * state + end
        out_ref[8 * pair : 8 * (pair + 1), :] = jnp.concatenate(held, axis=0)


def prefix(got):
    return pl.pallas_call(
        prefix_kernel,
        out_shape=jax.ShapeDtypeStruct((got.shape[0] // 2, LANES), F32),
        in_specs=[VMEM],
        out_specs=VMEM,
        name="prefix",
    )(got)


def back_kernel(
    g_ref, cum_ref, y_ref, mixed_ref, gain_ref, decay_ref, in_ref, out_ref, tot_ref, bc_ref, rate_ref
):
    rows, width = mixed_ref.shape
    tiles = width // LANES
    fold_rates(decay_ref, rate_ref)
    spread(g_ref[:, DT_RANK : DT_RANK + 2 * STATE].astype(F32), STATE, STATE, bc_ref)
    unroll = 8

    def group(i, carry):
        t0 = pl.multiple_of(i * unroll, unroll)
        for r in range(unroll):
            at = pl.ds(pl.multiple_of((t0 + r) * tiles, tiles), tiles)
            cum, y = cum_ref[at, :], y_ref[at, :]
            for n in range(STATE):
                of = slice(tiles * n, tiles * (n + 1))
                read = jnp.broadcast_to(bc_ref[n, pl.ds(t0 + r, 1), :], cum.shape)
                y = y + jnp.exp2(cum * rate_ref[of, :]) * (in_ref[of, :] * read)
            tot_ref[at, :] = y
        return carry

    lax.fori_loop(0, rows // unroll, group, 0)
    for j in range(tiles):
        c = slice(LANES * j, LANES * (j + 1))
        direct = gain_ref[:, c] * mixed_ref[:, c].astype(F32)
        out_ref[:, c] = (tot_ref[pl.ds(j, rows, tiles), :] + direct).astype(BF16)


def back(g, cum, y, mixed, gain, decay, incoming):
    rows, width = mixed.shape
    return pl.pallas_call(
        back_kernel,
        out_shape=jax.ShapeDtypeStruct((rows, width), BF16),
        in_specs=[VMEM] * 7,
        out_specs=VMEM,
        scratch_shapes=[
            pltpu.VMEM(cum.shape, F32),
            pltpu.VMEM((STATE, rows, LANES), F32),
            pltpu.VMEM(incoming.shape, F32),
        ],
        compiler_params=PARAMS,
        name="back",
    )(g, cum, y, mixed, gain, decay, incoming)


def shards(inputs, conv_weight, conv_bias, proj_weight, dt_weight, dt_bias, decay_rate, skip_gain):
    rows, width = inputs.shape
    seq, mp = lax.axis_size("seq"), lax.axis_size("mp")
    halo = lax.ppermute(inputs[rows - 8 :], "seq", [(s, s + 1) for s in range(seq - 1)])
    mixed, part = front(
        inputs, halo, conv_weight, conv_bias.reshape(1, width), jnp.transpose(proj_weight)
    )
    parts = lax.all_to_all(part, "mp", 0, 0, tiled=True)
    own = jnp.sum(parts.reshape(mp, rows // mp, part.shape[1]).astype(F32), axis=0).astype(BF16)
    projected = lax.all_gather(own, "mp", axis=0, tiled=True)
    decay = jnp.transpose(decay_rate)
    y, cum, send = scan(projected, dt_weight, dt_bias.reshape(1, width), mixed, decay)
    got = lax.all_to_all(send, "seq", 0, 0, tiled=True)
    incoming = lax.all_to_all(prefix(got), "seq", 0, 0, tiled=True)
    return back(projected, cum, y, mixed, skip_gain.reshape(1, width), decay, incoming)


def solution(mesh):
    placed = (
        P("seq", "mp"),
        P(None, "mp"),
        P("mp"),
        P("mp", None),
        P(None, "mp"),
        P("mp"),
        P("mp", None),
        P("mp"),
    )
    return jax.shard_map(
        shards, mesh=mesh, in_specs=placed, out_specs=P("seq", "mp"), check_vma=False
    )
```

```python
import jax
import jax.numpy as jnp
from jax import lax
from jax.experimental import pallas as pl
from jax.experimental.pallas import tpu as pltpu
from jax.sharding import PartitionSpec as P

F32, BF16 = jnp.float32, jnp.bfloat16
STATE = 16
DT_RANK = 512
LANES, TILES = 128, 8
LOG2E = 1.4426950408889634
PACK = STATE * TILES + 2 * TILES
Z = 8
UNROLL = 8
VMEM = pl.BlockSpec(memory_space=pltpu.VMEM)


def params(mib):
    return pltpu.CompilerParams(vmem_limit_bytes=mib << 20)


def cost(flops):
    return pl.CostEstimate(flops=flops, bytes_accessed=flops // 4, transcendentals=flops // 8)


def taps(pad_ref, w_ref, b_ref, first, count):
    pre = b_ref[...] + w_ref[0:1, :] * pad_ref[first + 5 : first + 5 + count, :]
    for k in range(1, 4):
        pre = pre + w_ref[k : k + 1, :] * pad_ref[first + 5 + k : first + 5 + k + count, :]
    return pre / (1.0 + jnp.exp(-pre))


def mix_kernel(
    x_hbm, w_hbm, b_hbm, pw_hbm, dtw_hbm, dtb_hbm, decay_hbm, gain_hbm,
    mixed_ref, head_ref, w_ref, b_ref, pw_ref, dtw_ref, dtb_ref, rate_ref, gain_ref,
    x_ref, pad_ref, decay_ref, row_ref, sems,
):
    rows = x_hbm.shape[0]
    step, parts = 16, 4
    some = rows // parts
    small = [
        pltpu.make_async_copy(source, target, sems.at[i])
        for i, (source, target) in enumerate(((w_hbm, w_ref), (b_hbm, b_ref)))
    ]
    chunks = [
        pltpu.make_async_copy(x_hbm.at[pl.ds(some * i, some)], x_ref.at[pl.ds(some * i, some)], sems.at[2 + i])
        for i in range(parts)
    ]
    later = [
        pltpu.make_async_copy(source, target, sems.at[2 + parts + i])
        for i, (source, target) in enumerate(
            ((decay_hbm, decay_ref), (gain_hbm, row_ref), (pw_hbm, pw_ref), (dtw_hbm, dtw_ref), (dtb_hbm, dtb_ref))
        )
    ]
    for copy in small + chunks + later:
        copy.start()
    pad_ref[0:8, :] = jnp.zeros_like(pad_ref[0:8, :])
    for copy in small:
        copy.wait()
    for i, copy in enumerate(chunks):
        copy.wait()
        for r in range(some * i, some * (i + 1), step):
            pad_ref[8 + r : 8 + r + step, :] = x_ref[r : r + step, :].astype(F32)
            mixed_ref[r : r + step, :] = taps(pad_ref, w_ref, b_ref, r, step).astype(BF16)
    head_ref[...] = pad_ref[8:16, :]
    for copy in later:
        copy.wait()
    for j in range(TILES):
        c = slice(LANES * j, LANES * (j + 1))
        rate_ref[pl.ds(j, STATE, TILES), :] = decay_ref[:, c] * -LOG2E
        gain_ref[j : j + 1, :] = row_ref[:, c]


def mix(x, weight, bias, weight_t, dtw, dtb, decay, gain):
    rows, width = x.shape
    return pl.pallas_call(
        mix_kernel,
        out_shape=(
            pltpu.VMEM((rows, width), BF16),
            pltpu.VMEM((8, width), F32),
            pltpu.VMEM(weight.shape, F32),
            pltpu.VMEM(bias.shape, F32),
            pltpu.VMEM(weight_t.shape, BF16),
            pltpu.VMEM(dtw.shape, BF16),
            pltpu.VMEM(dtb.shape, F32),
            pltpu.VMEM((STATE * TILES, LANES), F32),
            pltpu.VMEM((TILES, LANES), F32),
        ),
        in_specs=[pl.BlockSpec(memory_space=pltpu.HBM)] * 8,
        out_specs=(VMEM,) * 9,
        scratch_shapes=[
            pltpu.VMEM((rows, width), BF16),
            pltpu.VMEM((rows + 8, width), F32),
            pltpu.VMEM(decay.shape, F32),
            pltpu.VMEM(gain.shape, F32),
            pltpu.SemaphoreType.DMA((11,)),
        ],
        compiler_params=params(60),
        cost_estimate=cost(20_000_000),
        name="mix",
    )(x, weight, bias, weight_t, dtw, dtb, decay, gain)


def project_kernel(first_ref, head_ref, halo_ref, w_ref, b_ref, pw_ref, mixed_ref, part_ref, pad_ref):
    pad_ref[0:8, :] = halo_ref[...].astype(F32)
    pad_ref[8:16, :] = head_ref[...]
    top = taps(pad_ref, w_ref, b_ref, 0, 8)
    mixed_ref[16:, :] = first_ref[16:, :]
    mixed_ref[0:16, :] = jnp.concatenate([top, first_ref[0:16, :].astype(F32)[8:16]], axis=0).astype(BF16)
    share = lax.dot_general(
        mixed_ref[...], pw_ref[...], (((1,), (1,)), ((), ())), preferred_element_type=F32
    ).astype(BF16)
    pairs = share.shape[0] // 32
    for to in range(2 * pairs):
        at = 16 * ((to % 2) * pairs + to // 2)
        part_ref[16 * to : 16 * (to + 1), :] = share[at : at + 16, :]


def project(first, head, halo, weight, bias, weight_t):
    rows, width = first.shape
    return pl.pallas_call(
        project_kernel,
        out_shape=(
            pltpu.VMEM((rows, width), BF16),
            jax.ShapeDtypeStruct((rows, weight_t.shape[0]), BF16),
        ),
        in_specs=[VMEM] * 6,
        out_specs=(VMEM,) * 2,
        scratch_shapes=[pltpu.VMEM((16, width), F32)],
        compiler_params=params(8),
        name="project",
    )(first, head, halo, weight, bias, weight_t)


def total_kernel(parts_ref, out_ref):
    rows = 16
    total = parts_ref[0:rows, :].astype(F32)
    for k in range(1, parts_ref.shape[0] // rows):
        total = total + parts_ref[rows * k : rows * (k + 1), :].astype(F32)
    for k in range(out_ref.shape[0] // rows):
        out_ref[rows * k : rows * (k + 1), :] = total.astype(BF16)


def total(parts):
    return pl.pallas_call(
        total_kernel,
        out_shape=jax.ShapeDtypeStruct((parts.shape[0] // 2, parts.shape[1]), BF16),
        in_specs=[VMEM],
        out_specs=VMEM,
        compiler_params=params(8),
        name="total",
    )(parts)


def spread(columns, first, count, out_ref):
    for n in range(count):
        out_ref[n] = jnp.broadcast_to(
            columns[:, first + n : first + n + 1], (columns.shape[0], LANES)
        )


def tile(n):
    return slice(TILES * n, TILES * (n + 1))


def token(t):
    return pl.ds(pl.multiple_of(t * TILES, TILES), TILES)


def split_sum(value):
    high = value.astype(BF16).astype(F32)
    return jnp.concatenate([high, value - high], axis=0)


def sums_of(got_ref, k):
    both = got_ref[PACK * (k + 1) - 2 * TILES : PACK * (k + 1), :].astype(F32)
    return both[:TILES] + both[TILES:]


def states_of(got_ref, k, n):
    return got_ref[PACK * k + TILES * n : PACK * k + TILES * (n + 2), :].astype(F32)


def state_kernel(
    g_ref, dtw_ref, dtb_ref, mixed_ref, rate_ref, dt_hbm, send_ref, dt_ref, dx_ref, bc_ref, sem
):
    rows, width = mixed_ref.shape
    low = g_ref[:, 0:DT_RANK]
    for c in range(0, width, 256):
        pre = jnp.dot(low, dtw_ref[:, c : c + 256], preferred_element_type=F32)
        pre = pre + dtb_ref[:, c : c + 256]
        dt = jnp.maximum(pre, 0.0) + jnp.log1p(jnp.exp(-jnp.abs(pre)))
        dx = dt * mixed_ref[:, c : c + 256].astype(F32)
        for h in range(2):
            at = pl.ds(c // LANES + h, rows, TILES)
            dt_ref[at, :] = dt[:, LANES * h : LANES * (h + 1)]
            dx_ref[at, :] = dx[:, LANES * h : LANES * (h + 1)]
    keep = pltpu.make_async_copy(dt_ref, dt_hbm, sem)
    keep.start()
    spread(g_ref[:, DT_RANK : DT_RANK + 2 * STATE].astype(F32), 0, STATE, bc_ref)

    def group(i, carry):
        states, total = list(carry[:STATE]), carry[STATE]
        t0 = pl.multiple_of(i * UNROLL, UNROLL)
        for r in range(UNROLL):
            dt, dx = dt_ref[token(t0 + r), :], dx_ref[token(t0 + r), :]
            total = total + dt
            for n in range(STATE):
                enter = jnp.broadcast_to(bc_ref[n, pl.ds(t0 + r, 1), :], dt.shape)
                states[n] = jnp.exp2(dt * rate_ref[tile(n), :]) * states[n] + dx * enter
        return (*states, total)

    zero = jnp.zeros((TILES, LANES), F32)
    final = lax.fori_loop(0, rows // UNROLL, group, (zero,) * (STATE + 1))
    pack = [jnp.concatenate(final[n : n + 2], axis=0).astype(BF16) for n in range(0, STATE, 2)]
    pack.append(split_sum(final[STATE]).astype(BF16))
    for k in range(send_ref.shape[0] // PACK):
        for i, piece in enumerate(pack):
            at = PACK * k + 2 * TILES * i
            send_ref[at : at + 2 * TILES, :] = piece
    keep.wait()


def state(g, dtw, dtb, mixed, rate):
    rows, width = mixed.shape
    return pl.pallas_call(
        state_kernel,
        out_shape=(
            pltpu.HBM((rows * TILES, LANES), F32),
            jax.ShapeDtypeStruct((Z * PACK, LANES), BF16),
        ),
        in_specs=[VMEM] * 5,
        out_specs=(pl.BlockSpec(memory_space=pltpu.HBM), VMEM),
        scratch_shapes=[
            pltpu.VMEM((rows * TILES, LANES), F32),
            pltpu.VMEM((rows * TILES, LANES), F32),
            pltpu.VMEM((STATE, rows, LANES), F32),
            pltpu.SemaphoreType.DMA,
        ],
        compiler_params=params(12),
        name="state",
    )(g, dtw, dtb, mixed, rate)


def local_kernel(
    g_ref, dt_ref, rate_ref, mixed_ref, gain_ref, y_ref, cum_ref, rate_out, x_ref, bc_ref
):
    rows = mixed_ref.shape[0]
    rate_out[...] = rate_ref[...]
    spread(g_ref[:, DT_RANK : DT_RANK + 2 * STATE].astype(F32), 0, 2 * STATE, bc_ref)
    for j in range(TILES):
        x_ref[pl.ds(j, rows, TILES), :] = mixed_ref[:, LANES * j : LANES * (j + 1)].astype(F32)

    def group(i, carry):
        states, total = list(carry[:STATE]), carry[STATE]
        t0 = pl.multiple_of(i * UNROLL, UNROLL)
        for r in range(UNROLL):
            t = t0 + r
            dt, x = dt_ref[token(t), :], x_ref[token(t), :]
            dx, y = dt * x, gain_ref[...] * x
            total = total + dt
            cum_ref[token(t), :] = total
            for n in range(STATE):
                enter = jnp.broadcast_to(bc_ref[n, pl.ds(t, 1), :], dt.shape)
                read = jnp.broadcast_to(bc_ref[STATE + n, pl.ds(t, 1), :], dt.shape)
                states[n] = jnp.exp2(dt * rate_ref[tile(n), :]) * states[n] + dx * enter
                y = y + states[n] * read
            y_ref[token(t), :] = y
        return (*states, total)

    zero = jnp.zeros((TILES, LANES), F32)
    lax.fori_loop(0, rows // UNROLL, group, (zero,) * (STATE + 1))


def local(g, dt, rate, mixed, gain):
    rows = mixed.shape[0]
    flat = pltpu.VMEM((rows * TILES, LANES), F32)
    return pl.pallas_call(
        local_kernel,
        out_shape=(flat, flat, pltpu.VMEM(rate.shape, F32)),
        in_specs=[VMEM] * 5,
        out_specs=(VMEM,) * 3,
        scratch_shapes=[flat, pltpu.VMEM((2 * STATE, rows, LANES), F32)],
        compiler_params=params(12),
        cost_estimate=cost(60_000_000),
        name="local",
    )(g, dt, rate, mixed, gain)


def merge_kernel(place_ref, got_ref, rate_ref, send_ref, state_ref, sum_ref):
    rows, count = send_ref.shape[0] // PACK, got_ref.shape[0] // PACK
    z, x = place_ref[0], place_ref[1]
    zero = jnp.zeros((TILES, LANES), F32)
    sums = [sums_of(got_ref, k) for k in range(count)]
    whole, before = zero, zero
    for k in range(count):
        whole = whole + sums[k]
        before = before + jnp.where(k < z, sums[k], 0.0)
    sum_ref[...] = before
    for n in range(0, STATE, 2):
        blocks = [states_of(got_ref, k, n) for k in range(count)]
        ends, held = [], []
        for h in range(2):
            run, keep = zero, zero
            for k in range(count):
                keep = jnp.where(k == z, run, keep)
                run = jnp.exp2(sums[k] * rate_ref[tile(n + h), :]) * run + blocks[k][tile(h)]
            ends.append(run)
            held.append(keep)
        state_ref[TILES * n : TILES * (n + 2), :] = jnp.concatenate(held, axis=0)
        both = jnp.concatenate(ends, axis=0)
        for d in range(rows):
            at = PACK * d + TILES * n
            send_ref[at : at + 2 * TILES, :] = jnp.where(d > x, both, 0.0).astype(BF16)
    both = split_sum(whole)
    for d in range(rows):
        send_ref[PACK * (d + 1) - 2 * TILES : PACK * (d + 1), :] = jnp.where(d > x, both, 0.0).astype(BF16)


def merge(place, got, rate, rows):
    return pl.pallas_call(
        merge_kernel,
        out_shape=(
            jax.ShapeDtypeStruct((rows * PACK, LANES), BF16),
            pltpu.VMEM((STATE * TILES, LANES), F32),
            pltpu.VMEM((TILES, LANES), F32),
        ),
        in_specs=[pl.BlockSpec(memory_space=pltpu.SMEM), VMEM, VMEM],
        out_specs=(VMEM,) * 3,
        compiler_params=params(8),
        name="merge",
    )(place, got, rate)


def finish_kernel(got_ref, state_ref, sum_ref, rate_ref, g_ref, y_ref, cum_ref, out_ref, tot_ref, bc_ref):
    rows = out_ref.shape[0]
    spread(g_ref[:, DT_RANK : DT_RANK + 2 * STATE].astype(F32), STATE, STATE, bc_ref)
    count = got_ref.shape[0] // PACK - 1
    sums = [sums_of(got_ref, k) for k in range(count)]
    incoming = []
    for n in range(0, STATE, 2):
        blocks = [states_of(got_ref, k, n) for k in range(count)]
        for h in range(2):
            rate = rate_ref[tile(n + h), :]
            run = blocks[0][tile(h)]
            for k in range(1, count):
                run = jnp.exp2(sums[k] * rate) * run + blocks[k][tile(h)]
            incoming.append(jnp.exp2(sum_ref[...] * rate) * run + state_ref[tile(n + h), :])

    def group(i, carry):
        t0 = pl.multiple_of(i * UNROLL, UNROLL)
        for r in range(UNROLL):
            t = t0 + r
            cum, y = cum_ref[token(t), :], y_ref[token(t), :]
            for n in range(STATE):
                read = jnp.broadcast_to(bc_ref[n, pl.ds(t, 1), :], cum.shape)
                y = y + jnp.exp2(cum * rate_ref[tile(n), :]) * (carry[n] * read)
            tot_ref[token(t), :] = y
        return carry

    lax.fori_loop(0, rows // UNROLL, group, tuple(incoming))
    for j in range(TILES):
        out_ref[:, LANES * j : LANES * (j + 1)] = tot_ref[pl.ds(j, rows, TILES), :].astype(BF16)


def finish(got, states, sums, rate, g, y, cum):
    rows = g.shape[0]
    return pl.pallas_call(
        finish_kernel,
        out_shape=jax.ShapeDtypeStruct((rows, TILES * LANES), BF16),
        in_specs=[VMEM] * 7,
        out_specs=VMEM,
        scratch_shapes=[pltpu.VMEM(y.shape, F32), pltpu.VMEM((STATE, rows, LANES), F32)],
        compiler_params=params(8),
        name="finish",
    )(got, states, sums, rate, g, y, cum)


def shards(inputs, conv_weight, conv_bias, proj_weight, dt_weight, dt_bias, decay_rate, skip_gain):
    rows, width = inputs.shape
    seq, mp = lax.axis_size("seq"), lax.axis_size("mp")
    x_size, y_size = seq // Z, mp // 2
    on_z = [[Z * x + z for z in range(Z)] for x in range(x_size)]
    on_x = [[Z * x + z for x in range(x_size)] for z in range(Z)]
    on_y = [[2 * y + core for y in range(y_size)] for core in range(2)]
    on_chip = [[2 * y, 2 * y + 1] for y in range(y_size)]
    me = lax.axis_index("seq")
    place = jnp.stack([me % Z, me // Z]).astype(jnp.int32)
    halo = lax.ppermute(inputs[rows - 8 :], "seq", [(s, s + 1) for s in range(seq - 1)])
    first, head, taps_in, bias, weight, dtw, dtb, rate, gain = mix(
        inputs,
        conv_weight,
        conv_bias.reshape(1, width),
        jnp.transpose(proj_weight),
        dt_weight,
        dt_bias.reshape(1, width),
        jnp.transpose(decay_rate),
        skip_gain.reshape(1, width),
    )
    mixed, part = project(first, head, halo, taps_in, bias, weight)
    parts = lax.all_to_all(part, "mp", 0, 0, tiled=True)
    mine = lax.all_to_all(total(parts), "mp", 0, 0, tiled=True, axis_index_groups=on_y)
    projected = lax.all_gather(mine, "mp", axis=0, tiled=True, axis_index_groups=on_chip)
    dt, ends = state(projected, dtw, dtb, mixed, rate)
    got = lax.all_to_all(ends, "seq", 0, 0, tiled=True, axis_index_groups=on_z)
    y, cum, rate = local(projected, dt, rate, mixed, gain)
    ends, states, sums = merge(place, got, rate, x_size)
    got = lax.all_to_all(ends, "seq", 0, 0, tiled=True, axis_index_groups=on_x)
    return finish(got, states, sums, rate, projected, y, cum)


def solution(mesh):
    placed = (
        P("seq", "mp"),
        P(None, "mp"),
        P("mp"),
        P("mp", None),
        P(None, "mp"),
        P("mp"),
        P("mp", None),
        P("mp"),
    )
    return jax.shard_map(
        shards, mesh=mesh, in_specs=placed, out_specs=P("seq", "mp"), check_vma=False
    )
```

```python
import jax
import jax.numpy as jnp
from jax import lax
from jax.experimental import pallas as pl
from jax.experimental.pallas import tpu as pltpu
from jax.sharding import PartitionSpec as P

F32, BF16 = jnp.float32, jnp.bfloat16
STATE = 16
DT_RANK = 512
LANES, TILES = 128, 8
LOG2E = 1.4426950408889634
PACK = STATE * TILES + 2 * TILES
Z = 8
UNROLL = 16
VMEM = pl.BlockSpec(memory_space=pltpu.VMEM)
SMEM = pl.BlockSpec(memory_space=pltpu.SMEM)


def params(mib):
    return pltpu.CompilerParams(vmem_limit_bytes=mib << 20)


def cost(flops):
    return pl.CostEstimate(flops=flops, bytes_accessed=flops // 4, transcendentals=flops // 8)


def taps(pad_ref, w_ref, b_ref, first, count):
    pre = b_ref[...] + w_ref[0:1, :] * pad_ref[first + 5 : first + 5 + count, :]
    for k in range(1, 4):
        pre = pre + w_ref[k : k + 1, :] * pad_ref[first + 5 + k : first + 5 + k + count, :]
    return pre / (1.0 + jnp.exp(-pre))


def mix_kernel(
    x_hbm, w_hbm, b_hbm, pw_hbm, dtw_hbm, dtb_hbm, decay_hbm, gain_hbm,
    mixed_ref, head_ref, w_ref, b_ref, pw_ref, dtw_ref, dtb_ref, rate_ref, gain_ref,
    x_ref, pad_ref, decay_ref, row_ref, sems,
):
    rows = x_hbm.shape[0]
    step, parts = 16, 4
    some = rows // parts
    small = [
        pltpu.make_async_copy(source, target, sems.at[i])
        for i, (source, target) in enumerate(((w_hbm, w_ref), (b_hbm, b_ref)))
    ]
    chunks = [
        pltpu.make_async_copy(x_hbm.at[pl.ds(some * i, some)], x_ref.at[pl.ds(some * i, some)], sems.at[2 + i])
        for i in range(parts)
    ]
    later = [
        pltpu.make_async_copy(source, target, sems.at[2 + parts + i])
        for i, (source, target) in enumerate(
            ((decay_hbm, decay_ref), (gain_hbm, row_ref), (pw_hbm, pw_ref), (dtw_hbm, dtw_ref), (dtb_hbm, dtb_ref))
        )
    ]
    for copy in small + chunks + later:
        copy.start()
    pad_ref[0:8, :] = jnp.zeros_like(pad_ref[0:8, :])
    for copy in small:
        copy.wait()
    for i, copy in enumerate(chunks):
        copy.wait()
        for r in range(some * i, some * (i + 1), step):
            pad_ref[8 + r : 8 + r + step, :] = x_ref[r : r + step, :].astype(F32)
            mixed_ref[r : r + step, :] = taps(pad_ref, w_ref, b_ref, r, step).astype(BF16)
    head_ref[...] = pad_ref[8:16, :]
    for copy in later:
        copy.wait()
    for j in range(TILES):
        c = slice(LANES * j, LANES * (j + 1))
        rate_ref[pl.ds(j, STATE, TILES), :] = decay_ref[:, c] * -LOG2E
        gain_ref[j : j + 1, :] = row_ref[:, c]


def mix(x, weight, bias, weight_t, dtw, dtb, decay, gain):
    rows, width = x.shape
    return pl.pallas_call(
        mix_kernel,
        out_shape=(
            pltpu.VMEM((rows, width), BF16),
            pltpu.VMEM((8, width), F32),
            pltpu.VMEM(weight.shape, F32),
            pltpu.VMEM(bias.shape, F32),
            pltpu.VMEM(weight_t.shape, BF16),
            pltpu.VMEM(dtw.shape, BF16),
            pltpu.VMEM(dtb.shape, F32),
            pltpu.VMEM((STATE * TILES, LANES), F32),
            pltpu.VMEM((TILES, LANES), F32),
        ),
        in_specs=[pl.BlockSpec(memory_space=pltpu.HBM)] * 8,
        out_specs=(VMEM,) * 9,
        scratch_shapes=[
            pltpu.VMEM((rows, width), BF16),
            pltpu.VMEM((rows + 8, width), F32),
            pltpu.VMEM(decay.shape, F32),
            pltpu.VMEM(gain.shape, F32),
            pltpu.SemaphoreType.DMA((11,)),
        ],
        compiler_params=params(60),
        cost_estimate=cost(20_000_000),
        name="mix",
    )(x, weight, bias, weight_t, dtw, dtb, decay, gain)


def project_kernel(
    place_ref, first_ref, head_ref, halo_ref, w_ref, b_ref, pw_ref, mixed_ref, share_ref, send_ref, pad_ref
):
    pad_ref[0:8, :] = halo_ref[...].astype(F32)
    pad_ref[8:16, :] = head_ref[...]
    top = taps(pad_ref, w_ref, b_ref, 0, 8)
    mixed_ref[16:, :] = first_ref[16:, :]
    mixed_ref[0:16, :] = jnp.concatenate([top, first_ref[0:16, :].astype(F32)[8:16]], axis=0).astype(BF16)
    share_ref[...] = lax.dot_general(
        mixed_ref[...], pw_ref[...], (((1,), (1,)), ((), ())), preferred_element_type=F32
    )
    half = send_ref.shape[0]
    theirs = pl.multiple_of((1 - place_ref[2]) * half, half)
    send_ref[...] = share_ref[pl.ds(theirs, half), :].astype(BF16)


def project(place, first, head, halo, weight, bias, weight_t):
    rows, width = first.shape
    columns = weight_t.shape[0]
    return pl.pallas_call(
        project_kernel,
        out_shape=(
            pltpu.VMEM((rows, width), BF16),
            pltpu.VMEM((rows, columns), F32),
            jax.ShapeDtypeStruct((rows // 2, columns), BF16),
        ),
        in_specs=[SMEM] + [VMEM] * 6,
        out_specs=(VMEM,) * 3,
        scratch_shapes=[pltpu.VMEM((16, width), F32)],
        compiler_params=params(8),
        name="project",
    )(place, first, head, halo, weight, bias, weight_t)


def pair_kernel(place_ref, share_ref, got_ref, out_ref):
    half = out_ref.shape[0]
    ours = pl.multiple_of(place_ref[2] * half, half)
    theirs = pl.multiple_of((1 - place_ref[2]) * half, half)
    out_ref[...] = (share_ref[pl.ds(ours, half), :] + got_ref[pl.ds(theirs, half), :].astype(F32)).astype(BF16)


def pair(place, share, got):
    return pl.pallas_call(
        pair_kernel,
        out_shape=jax.ShapeDtypeStruct((share.shape[0] // 2, share.shape[1]), BF16),
        in_specs=[SMEM] + [VMEM] * 2,
        out_specs=VMEM,
        compiler_params=params(8),
        name="pair",
    )(place, share, got)


def total_kernel(parts_ref, out_ref):
    rows = 16
    total = parts_ref[0:rows, :].astype(F32)
    for k in range(1, parts_ref.shape[0] // rows):
        total = total + parts_ref[rows * k : rows * (k + 1), :].astype(F32)
    for k in range(out_ref.shape[0] // rows):
        out_ref[rows * k : rows * (k + 1), :] = total.astype(BF16)


def total(parts):
    return pl.pallas_call(
        total_kernel,
        out_shape=jax.ShapeDtypeStruct(parts.shape, BF16),
        in_specs=[VMEM],
        out_specs=VMEM,
        compiler_params=params(8),
        name="total",
    )(parts)


def spread(columns, first, count, out_ref):
    for n in range(count):
        out_ref[n] = jnp.broadcast_to(
            columns[:, first + n : first + n + 1], (columns.shape[0], LANES)
        )


def tile(n):
    return slice(TILES * n, TILES * (n + 1))


def token(t):
    return pl.ds(pl.multiple_of(t * TILES, TILES), TILES)


def split_sum(value):
    high = value.astype(BF16).astype(F32)
    return jnp.concatenate([high, value - high], axis=0)


def sums_of(got_ref, k):
    both = got_ref[PACK * (k + 1) - 2 * TILES : PACK * (k + 1), :].astype(F32)
    return both[:TILES] + both[TILES:]


def states_of(got_ref, k, n):
    return got_ref[PACK * k + TILES * n : PACK * k + TILES * (n + 2), :].astype(F32)


def state_kernel(
    g_ref, dtw_ref, dtb_ref, mixed_ref, rate_ref, dt_hbm, send_ref, dt_ref, dx_ref, bc_ref, sem
):
    rows, width = mixed_ref.shape
    low = g_ref[:, 0:DT_RANK]
    for c in range(0, width, 256):
        pre = jnp.dot(low, dtw_ref[:, c : c + 256], preferred_element_type=F32)
        pre = pre + dtb_ref[:, c : c + 256]
        small = jnp.exp(-jnp.abs(pre))
        log1p = jnp.where(small < 1e-3, small - 0.5 * small * small, jnp.log(1.0 + small))
        dt = jnp.maximum(pre, 0.0) + log1p
        dx = dt * mixed_ref[:, c : c + 256].astype(F32)
        for h in range(2):
            at = pl.ds(c // LANES + h, rows, TILES)
            dt_ref[at, :] = dt[:, LANES * h : LANES * (h + 1)]
            dx_ref[at, :] = dx[:, LANES * h : LANES * (h + 1)]
    keep = pltpu.make_async_copy(dt_ref, dt_hbm, sem)
    keep.start()
    spread(g_ref[:, DT_RANK : DT_RANK + 2 * STATE].astype(F32), 0, STATE, bc_ref)

    def group(i, carry):
        states, total = list(carry[:STATE]), carry[STATE]
        t0 = pl.multiple_of(i * UNROLL, UNROLL)
        for r in range(UNROLL):
            dt, dx = dt_ref[token(t0 + r), :], dx_ref[token(t0 + r), :]
            total = total + dt
            for n in range(STATE):
                enter = jnp.broadcast_to(bc_ref[n, pl.ds(t0 + r, 1), :], dt.shape)
                states[n] = jnp.exp2(dt * rate_ref[tile(n), :]) * states[n] + dx * enter
        return (*states, total)

    zero = jnp.zeros((TILES, LANES), F32)
    final = lax.fori_loop(0, rows // UNROLL, group, (zero,) * (STATE + 1))
    pack = [jnp.concatenate(final[n : n + 2], axis=0).astype(BF16) for n in range(0, STATE, 2)]
    pack.append(split_sum(final[STATE]).astype(BF16))
    for k in range(send_ref.shape[0] // PACK):
        for i, piece in enumerate(pack):
            at = PACK * k + 2 * TILES * i
            send_ref[at : at + 2 * TILES, :] = piece
    keep.wait()


def state(g, dtw, dtb, mixed, rate):
    rows, width = mixed.shape
    return pl.pallas_call(
        state_kernel,
        out_shape=(
            pltpu.HBM((rows * TILES, LANES), F32),
            jax.ShapeDtypeStruct((Z * PACK, LANES), BF16),
        ),
        in_specs=[VMEM] * 5,
        out_specs=(pl.BlockSpec(memory_space=pltpu.HBM), VMEM),
        scratch_shapes=[
            pltpu.VMEM((rows * TILES, LANES), F32),
            pltpu.VMEM((rows * TILES, LANES), F32),
            pltpu.VMEM((STATE, rows, LANES), F32),
            pltpu.SemaphoreType.DMA,
        ],
        compiler_params=params(12),
        name="state",
    )(g, dtw, dtb, mixed, rate)


def local_kernel(
    g_ref, dt_ref, rate_ref, mixed_ref, gain_ref, y_ref, cum_ref, rate_out, x_ref, bc_ref
):
    rows = mixed_ref.shape[0]
    rate_out[...] = rate_ref[...]
    spread(g_ref[:, DT_RANK : DT_RANK + 2 * STATE].astype(F32), 0, 2 * STATE, bc_ref)
    for j in range(TILES):
        x_ref[pl.ds(j, rows, TILES), :] = mixed_ref[:, LANES * j : LANES * (j + 1)].astype(F32)

    def group(i, carry):
        states, total = list(carry[:STATE]), carry[STATE]
        t0 = pl.multiple_of(i * UNROLL, UNROLL)
        for r in range(UNROLL):
            t = t0 + r
            dt, x = dt_ref[token(t), :], x_ref[token(t), :]
            dx, y = dt * x, gain_ref[...] * x
            total = total + dt
            cum_ref[token(t), :] = total
            for n in range(STATE):
                enter = jnp.broadcast_to(bc_ref[n, pl.ds(t, 1), :], dt.shape)
                read = jnp.broadcast_to(bc_ref[STATE + n, pl.ds(t, 1), :], dt.shape)
                states[n] = jnp.exp2(dt * rate_ref[tile(n), :]) * states[n] + dx * enter
                y = y + states[n] * read
            y_ref[token(t), :] = y
        return (*states, total)

    zero = jnp.zeros((TILES, LANES), F32)
    lax.fori_loop(0, rows // UNROLL, group, (zero,) * (STATE + 1))


def local(g, dt, rate, mixed, gain):
    rows = mixed.shape[0]
    flat = pltpu.VMEM((rows * TILES, LANES), F32)
    return pl.pallas_call(
        local_kernel,
        out_shape=(flat, flat, pltpu.VMEM(rate.shape, F32)),
        in_specs=[VMEM] * 5,
        out_specs=(VMEM,) * 3,
        scratch_shapes=[flat, pltpu.VMEM((2 * STATE, rows, LANES), F32)],
        compiler_params=params(12),
        cost_estimate=cost(60_000_000),
        name="local",
    )(g, dt, rate, mixed, gain)


def merge_kernel(place_ref, got_ref, rate_ref, send_ref, state_ref, sum_ref):
    rows, count = send_ref.shape[0] // PACK, got_ref.shape[0] // PACK
    z, x = place_ref[0], place_ref[1]
    zero = jnp.zeros((TILES, LANES), F32)
    sums = [sums_of(got_ref, k) for k in range(count)]
    whole, before = zero, zero
    for k in range(count):
        whole = whole + sums[k]
        before = before + jnp.where(k < z, sums[k], 0.0)
    sum_ref[...] = before
    for n in range(0, STATE, 2):
        blocks = [states_of(got_ref, k, n) for k in range(count)]
        ends, held = [], []
        for h in range(2):
            run, keep = zero, zero
            for k in range(count):
                keep = jnp.where(k == z, run, keep)
                run = jnp.exp2(sums[k] * rate_ref[tile(n + h), :]) * run + blocks[k][tile(h)]
            ends.append(run)
            held.append(keep)
        state_ref[TILES * n : TILES * (n + 2), :] = jnp.concatenate(held, axis=0)
        both = jnp.concatenate(ends, axis=0)
        for d in range(rows):
            at = PACK * d + TILES * n
            send_ref[at : at + 2 * TILES, :] = jnp.where(d > x, both, 0.0).astype(BF16)
    both = split_sum(whole)
    for d in range(rows):
        send_ref[PACK * (d + 1) - 2 * TILES : PACK * (d + 1), :] = jnp.where(d > x, both, 0.0).astype(BF16)


def merge(place, got, rate, rows):
    return pl.pallas_call(
        merge_kernel,
        out_shape=(
            jax.ShapeDtypeStruct((rows * PACK, LANES), BF16),
            pltpu.VMEM((STATE * TILES, LANES), F32),
            pltpu.VMEM((TILES, LANES), F32),
        ),
        in_specs=[SMEM, VMEM, VMEM],
        out_specs=(VMEM,) * 3,
        compiler_params=params(8),
        name="merge",
    )(place, got, rate)


def finish_kernel(got_ref, state_ref, sum_ref, rate_ref, g_ref, y_ref, cum_ref, out_ref, tot_ref, bc_ref):
    rows = out_ref.shape[0]
    spread(g_ref[:, DT_RANK : DT_RANK + 2 * STATE].astype(F32), STATE, STATE, bc_ref)
    count = got_ref.shape[0] // PACK - 1
    sums = [sums_of(got_ref, k) for k in range(count)]
    incoming = []
    for n in range(0, STATE, 2):
        blocks = [states_of(got_ref, k, n) for k in range(count)]
        for h in range(2):
            rate = rate_ref[tile(n + h), :]
            run = blocks[0][tile(h)]
            for k in range(1, count):
                run = jnp.exp2(sums[k] * rate) * run + blocks[k][tile(h)]
            incoming.append(jnp.exp2(sum_ref[...] * rate) * run + state_ref[tile(n + h), :])

    def group(i, carry):
        t0 = pl.multiple_of(i * UNROLL, UNROLL)
        for r in range(UNROLL):
            t = t0 + r
            cum, y = cum_ref[token(t), :], y_ref[token(t), :]
            for n in range(STATE):
                read = jnp.broadcast_to(bc_ref[n, pl.ds(t, 1), :], cum.shape)
                y = y + jnp.exp2(cum * rate_ref[tile(n), :]) * (carry[n] * read)
            tot_ref[token(t), :] = y
        return carry

    lax.fori_loop(0, rows // UNROLL, group, tuple(incoming))
    for j in range(TILES):
        out_ref[:, LANES * j : LANES * (j + 1)] = tot_ref[pl.ds(j, rows, TILES), :].astype(BF16)


def finish(got, states, sums, rate, g, y, cum):
    rows = g.shape[0]
    return pl.pallas_call(
        finish_kernel,
        out_shape=jax.ShapeDtypeStruct((rows, TILES * LANES), BF16),
        in_specs=[VMEM] * 7,
        out_specs=VMEM,
        scratch_shapes=[pltpu.VMEM(y.shape, F32), pltpu.VMEM((STATE, rows, LANES), F32)],
        compiler_params=params(8),
        name="finish",
    )(got, states, sums, rate, g, y, cum)


def shards(inputs, conv_weight, conv_bias, proj_weight, dt_weight, dt_bias, decay_rate, skip_gain):
    rows, width = inputs.shape
    seq, mp = lax.axis_size("seq"), lax.axis_size("mp")
    x_size, y_size = seq // Z, mp // 2
    on_z = [[Z * x + z for z in range(Z)] for x in range(x_size)]
    on_x = [[Z * x + z for x in range(x_size)] for z in range(Z)]
    on_y = [[2 * y + core for y in range(y_size)] for core in range(2)]
    on_chip = [[2 * y, 2 * y + 1] for y in range(y_size)]
    me = lax.axis_index("seq")
    place = jnp.stack([me % Z, me // Z, lax.axis_index("mp") % 2]).astype(jnp.int32)
    halo = lax.ppermute(inputs[rows - 8 :], "seq", [(s, s + 1) for s in range(seq - 1)])
    first, head, taps_in, bias, weight, dtw, dtb, rate, gain = mix(
        inputs,
        conv_weight,
        conv_bias.reshape(1, width),
        jnp.transpose(proj_weight),
        dt_weight,
        dt_bias.reshape(1, width),
        jnp.transpose(decay_rate),
        skip_gain.reshape(1, width),
    )
    mixed, share, theirs = project(place, first, head, halo, taps_in, bias, weight)
    both = lax.all_gather(theirs, "mp", axis=0, tiled=True, axis_index_groups=on_chip)
    parts = lax.all_to_all(pair(place, share, both), "mp", 0, 0, tiled=True, axis_index_groups=on_y)
    mine = lax.all_to_all(total(parts), "mp", 0, 0, tiled=True, axis_index_groups=on_y)
    projected = lax.all_gather(mine, "mp", axis=0, tiled=True, axis_index_groups=on_chip)
    dt, ends = state(projected, dtw, dtb, mixed, rate)
    got = lax.all_to_all(ends, "seq", 0, 0, tiled=True, axis_index_groups=on_z)
    y, cum, rate = local(projected, dt, rate, mixed, gain)
    ends, states, sums = merge(place, got, rate, x_size)
    got = lax.all_to_all(ends, "seq", 0, 0, tiled=True, axis_index_groups=on_x)
    return finish(got, states, sums, rate, projected, y, cum)


def solution(mesh):
    placed = (
        P("seq", "mp"),
        P(None, "mp"),
        P("mp"),
        P("mp", None),
        P(None, "mp"),
        P("mp"),
        P("mp", None),
        P("mp"),
    )
    return jax.shard_map(
        shards, mesh=mesh, in_specs=placed, out_specs=P("seq", "mp"), check_vma=False
    )
```

```python
import jax
import jax.numpy as jnp
from jax import lax
from jax.experimental import pallas as pl
from jax.experimental.pallas import tpu as pltpu
from jax.sharding import PartitionSpec as P

F32, BF16 = jnp.float32, jnp.bfloat16
STATE = 16
DT_RANK = 512
LANES, TILES = 128, 8
LOG2E = 1.4426950408889634
PACK = STATE * TILES + 2 * TILES
Z = 8
UNROLL = 16
VMEM = pl.BlockSpec(memory_space=pltpu.VMEM)
SMEM = pl.BlockSpec(memory_space=pltpu.SMEM)


def params(mib):
    return pltpu.CompilerParams(vmem_limit_bytes=mib << 20)


def cost(flops):
    return pl.CostEstimate(flops=flops, bytes_accessed=flops // 4, transcendentals=flops // 8)


def taps(pad_ref, w_ref, b_ref, first, count):
    pre = b_ref[...] + w_ref[0:1, :] * pad_ref[first + 5 : first + 5 + count, :]
    for k in range(1, 4):
        pre = pre + w_ref[k : k + 1, :] * pad_ref[first + 5 + k : first + 5 + k + count, :]
    return pre / (1.0 + jnp.exp(-pre))


def multiply(rows, weight_t):
    return lax.dot_general(rows, weight_t, (((1,), (1,)), ((), ())), preferred_element_type=F32).astype(BF16)


def mix_kernel(
    x_hbm, w_hbm, b_hbm, pw_hbm, dtw_hbm, dtb_hbm, decay_hbm, gain_hbm,
    mixed_ref, head_ref, share_ref, w_ref, b_ref, pw_ref, dtw_ref, dtb_ref, rate_ref, gain_ref,
    x_ref, pad_ref, decay_ref, row_ref, sems,
):
    rows = x_hbm.shape[0]
    step, parts = 16, 4
    some = rows // parts
    small = [
        pltpu.make_async_copy(source, target, sems.at[i])
        for i, (source, target) in enumerate(((w_hbm, w_ref), (b_hbm, b_ref)))
    ]
    chunks = [
        pltpu.make_async_copy(x_hbm.at[pl.ds(some * i, some)], x_ref.at[pl.ds(some * i, some)], sems.at[2 + i])
        for i in range(parts)
    ]
    later = [
        pltpu.make_async_copy(source, target, sems.at[2 + parts + i])
        for i, (source, target) in enumerate(
            ((decay_hbm, decay_ref), (gain_hbm, row_ref), (pw_hbm, pw_ref), (dtw_hbm, dtw_ref), (dtb_hbm, dtb_ref))
        )
    ]
    for copy in small + chunks + later:
        copy.start()
    pad_ref[0:8, :] = jnp.zeros_like(pad_ref[0:8, :])
    for copy in small:
        copy.wait()
    for i, copy in enumerate(chunks):
        copy.wait()
        for r in range(some * i, some * (i + 1), step):
            pad_ref[8 + r : 8 + r + step, :] = x_ref[r : r + step, :].astype(F32)
            mixed_ref[r : r + step, :] = taps(pad_ref, w_ref, b_ref, r, step).astype(BF16)
    head_ref[...] = pad_ref[8:16, :]
    for copy in later:
        copy.wait()
    for j in range(TILES):
        c = slice(LANES * j, LANES * (j + 1))
        rate_ref[pl.ds(j, STATE, TILES), :] = decay_ref[:, c] * -LOG2E
        gain_ref[j : j + 1, :] = row_ref[:, c]
    share_ref[...] = multiply(mixed_ref[...], pw_ref[...])


def mix(x, weight, bias, weight_t, dtw, dtb, decay, gain):
    rows, width = x.shape
    return pl.pallas_call(
        mix_kernel,
        out_shape=(
            pltpu.VMEM((rows, width), BF16),
            pltpu.VMEM((8, width), F32),
            pltpu.VMEM((rows, weight_t.shape[0]), BF16),
            pltpu.VMEM(weight.shape, F32),
            pltpu.VMEM(bias.shape, F32),
            pltpu.VMEM(weight_t.shape, BF16),
            pltpu.VMEM(dtw.shape, BF16),
            pltpu.VMEM(dtb.shape, F32),
            pltpu.VMEM((STATE * TILES, LANES), F32),
            pltpu.VMEM((TILES, LANES), F32),
        ),
        in_specs=[pl.BlockSpec(memory_space=pltpu.HBM)] * 8,
        out_specs=(VMEM,) * 10,
        scratch_shapes=[
            pltpu.VMEM((rows, width), BF16),
            pltpu.VMEM((rows + 8, width), F32),
            pltpu.VMEM(decay.shape, F32),
            pltpu.VMEM(gain.shape, F32),
            pltpu.SemaphoreType.DMA((11,)),
        ],
        compiler_params=params(60),
        cost_estimate=cost(20_000_000),
        name="mix",
    )(x, weight, bias, weight_t, dtw, dtb, decay, gain)


def project_kernel(
    place_ref, first_ref, head_ref, share_ref, halo_ref, w_ref, b_ref, pw_ref, mixed_ref, ours_ref, theirs_ref, pad_ref, all_ref
):
    pad_ref[0:8, :] = halo_ref[...].astype(F32)
    pad_ref[8:16, :] = head_ref[...]
    top = taps(pad_ref, w_ref, b_ref, 0, 8)
    top = jnp.concatenate([top, first_ref[0:16, :].astype(F32)[8:16]], axis=0).astype(BF16)
    mixed_ref[16:, :] = first_ref[16:, :]
    mixed_ref[0:16, :] = top
    all_ref[16:, :] = share_ref[16:, :]
    all_ref[0:16, :] = multiply(top, pw_ref[...])
    half = ours_ref.shape[0]
    core = place_ref[2]
    ours_ref[...] = all_ref[pl.ds(pl.multiple_of(core * half, half), half), :]
    theirs_ref[...] = all_ref[pl.ds(pl.multiple_of((1 - core) * half, half), half), :]


def project(place, first, head, share, halo, weight, bias, weight_t):
    rows, width = first.shape
    half = pltpu.VMEM((rows // 2, share.shape[1]), BF16)
    return pl.pallas_call(
        project_kernel,
        out_shape=(pltpu.VMEM((rows, width), BF16), half, half),
        in_specs=[SMEM] + [VMEM] * 7,
        out_specs=(VMEM,) * 3,
        scratch_shapes=[pltpu.VMEM((16, width), F32), pltpu.VMEM(share.shape, BF16)],
        compiler_params=params(8),
        name="project",
    )(place, first, head, share, halo, weight, bias, weight_t)


def pair_kernel(place_ref, ours_ref, got_ref, out_ref):
    half = out_ref.shape[0]
    theirs = pl.multiple_of((1 - place_ref[2]) * half, half)
    out_ref[...] = (ours_ref[...].astype(F32) + got_ref[pl.ds(theirs, half), :].astype(F32)).astype(BF16)


def pair(place, ours, got):
    return pl.pallas_call(
        pair_kernel,
        out_shape=jax.ShapeDtypeStruct(ours.shape, BF16),
        in_specs=[SMEM] + [VMEM] * 2,
        out_specs=VMEM,
        compiler_params=params(8),
        name="pair",
    )(place, ours, got)


def total_kernel(parts_ref, out_ref):
    rows = 16
    total = parts_ref[0:rows, :].astype(F32)
    for k in range(1, parts_ref.shape[0] // rows):
        total = total + parts_ref[rows * k : rows * (k + 1), :].astype(F32)
    for k in range(out_ref.shape[0] // rows):
        out_ref[rows * k : rows * (k + 1), :] = total.astype(BF16)


def total(parts):
    return pl.pallas_call(
        total_kernel,
        out_shape=jax.ShapeDtypeStruct(parts.shape, BF16),
        in_specs=[VMEM],
        out_specs=VMEM,
        compiler_params=params(8),
        name="total",
    )(parts)


def spread(columns, first, count, out_ref):
    for n in range(count):
        out_ref[n] = jnp.broadcast_to(
            columns[:, first + n : first + n + 1], (columns.shape[0], LANES)
        )


def tile(n):
    return slice(TILES * n, TILES * (n + 1))


def token(t):
    return pl.ds(pl.multiple_of(t * TILES, TILES), TILES)


def split_sum(value):
    high = value.astype(BF16).astype(F32)
    return jnp.concatenate([high, value - high], axis=0)


def sums_of(got_ref, k):
    both = got_ref[PACK * (k + 1) - 2 * TILES : PACK * (k + 1), :].astype(F32)
    return both[:TILES] + both[TILES:]


def states_of(got_ref, k, n):
    return got_ref[PACK * k + TILES * n : PACK * k + TILES * (n + 2), :].astype(F32)


def state_kernel(
    g_ref, dtw_ref, dtb_ref, mixed_ref, rate_ref, dt_hbm, send_ref, dt_ref, dx_ref, bc_ref, sem
):
    rows, width = mixed_ref.shape
    low = g_ref[:, 0:DT_RANK]
    for c in range(0, width, 256):
        pre = jnp.dot(low, dtw_ref[:, c : c + 256], preferred_element_type=F32)
        pre = pre + dtb_ref[:, c : c + 256]
        small = jnp.exp(-jnp.abs(pre))
        log1p = jnp.where(small < 1e-3, small - 0.5 * small * small, jnp.log(1.0 + small))
        dt = jnp.maximum(pre, 0.0) + log1p
        dx = dt * mixed_ref[:, c : c + 256].astype(F32)
        for h in range(2):
            at = pl.ds(c // LANES + h, rows, TILES)
            dt_ref[at, :] = dt[:, LANES * h : LANES * (h + 1)]
            dx_ref[at, :] = dx[:, LANES * h : LANES * (h + 1)]
    keep = pltpu.make_async_copy(dt_ref, dt_hbm, sem)
    keep.start()
    spread(g_ref[:, DT_RANK : DT_RANK + 2 * STATE].astype(F32), 0, STATE, bc_ref)

    def group(i, carry):
        states, total = list(carry[:STATE]), carry[STATE]
        t0 = pl.multiple_of(i * UNROLL, UNROLL)
        for r in range(UNROLL):
            dt, dx = dt_ref[token(t0 + r), :], dx_ref[token(t0 + r), :]
            total = total + dt
            for n in range(STATE):
                enter = jnp.broadcast_to(bc_ref[n, pl.ds(t0 + r, 1), :], dt.shape)
                states[n] = jnp.exp2(dt * rate_ref[tile(n), :]) * states[n] + dx * enter
        return (*states, total)

    zero = jnp.zeros((TILES, LANES), F32)
    final = lax.fori_loop(0, rows // UNROLL, group, (zero,) * (STATE + 1))
    pack = [jnp.concatenate(final[n : n + 2], axis=0).astype(BF16) for n in range(0, STATE, 2)]
    pack.append(split_sum(final[STATE]).astype(BF16))
    for k in range(send_ref.shape[0] // PACK):
        for i, piece in enumerate(pack):
            at = PACK * k + 2 * TILES * i
            send_ref[at : at + 2 * TILES, :] = piece
    keep.wait()


def state(g, dtw, dtb, mixed, rate):
    rows, width = mixed.shape
    return pl.pallas_call(
        state_kernel,
        out_shape=(
            pltpu.HBM((rows * TILES, LANES), F32),
            pltpu.VMEM((Z * PACK, LANES), BF16),
        ),
        in_specs=[VMEM] * 5,
        out_specs=(pl.BlockSpec(memory_space=pltpu.HBM), VMEM),
        scratch_shapes=[
            pltpu.VMEM((rows * TILES, LANES), F32),
            pltpu.VMEM((rows * TILES, LANES), F32),
            pltpu.VMEM((STATE, rows, LANES), F32),
            pltpu.SemaphoreType.DMA,
        ],
        compiler_params=params(12),
        name="state",
    )(g, dtw, dtb, mixed, rate)


def local_kernel(
    g_ref, dt_ref, rate_ref, mixed_ref, gain_ref, y_ref, cum_ref, rate_out, x_ref, bc_ref
):
    rows = mixed_ref.shape[0]
    rate_out[...] = rate_ref[...]
    spread(g_ref[:, DT_RANK : DT_RANK + 2 * STATE].astype(F32), 0, 2 * STATE, bc_ref)
    for j in range(TILES):
        x_ref[pl.ds(j, rows, TILES), :] = mixed_ref[:, LANES * j : LANES * (j + 1)].astype(F32)

    def group(i, carry):
        states, total = list(carry[:STATE]), carry[STATE]
        t0 = pl.multiple_of(i * UNROLL, UNROLL)
        for r in range(UNROLL):
            t = t0 + r
            dt, x = dt_ref[token(t), :], x_ref[token(t), :]
            dx, y = dt * x, gain_ref[...] * x
            total = total + dt
            cum_ref[token(t), :] = total
            for n in range(STATE):
                enter = jnp.broadcast_to(bc_ref[n, pl.ds(t, 1), :], dt.shape)
                read = jnp.broadcast_to(bc_ref[STATE + n, pl.ds(t, 1), :], dt.shape)
                states[n] = jnp.exp2(dt * rate_ref[tile(n), :]) * states[n] + dx * enter
                y = y + states[n] * read
            y_ref[token(t), :] = y
        return (*states, total)

    zero = jnp.zeros((TILES, LANES), F32)
    lax.fori_loop(0, rows // UNROLL, group, (zero,) * (STATE + 1))


def local(g, dt, rate, mixed, gain):
    rows = mixed.shape[0]
    flat = pltpu.VMEM((rows * TILES, LANES), F32)
    return pl.pallas_call(
        local_kernel,
        out_shape=(flat, flat, pltpu.VMEM(rate.shape, F32)),
        in_specs=[VMEM] * 5,
        out_specs=(VMEM,) * 3,
        scratch_shapes=[flat, pltpu.VMEM((2 * STATE, rows, LANES), F32)],
        compiler_params=params(12),
        cost_estimate=cost(60_000_000),
        name="local",
    )(g, dt, rate, mixed, gain)


def merge_kernel(place_ref, got_ref, rate_ref, send_ref, state_ref, sum_ref):
    rows, count = send_ref.shape[0] // PACK, got_ref.shape[0] // PACK
    z, x = place_ref[0], place_ref[1]
    zero = jnp.zeros((TILES, LANES), F32)
    sums = [sums_of(got_ref, k) for k in range(count)]
    whole, before = zero, zero
    for k in range(count):
        whole = whole + sums[k]
        before = before + jnp.where(k < z, sums[k], 0.0)
    sum_ref[...] = before
    for n in range(0, STATE, 2):
        blocks = [states_of(got_ref, k, n) for k in range(count)]
        ends, held = [], []
        for h in range(2):
            run, keep = zero, zero
            for k in range(count):
                keep = jnp.where(k == z, run, keep)
                run = jnp.exp2(sums[k] * rate_ref[tile(n + h), :]) * run + blocks[k][tile(h)]
            ends.append(run)
            held.append(keep)
        state_ref[TILES * n : TILES * (n + 2), :] = jnp.concatenate(held, axis=0)
        both = jnp.concatenate(ends, axis=0)
        for d in range(rows):
            at = PACK * d + TILES * n
            send_ref[at : at + 2 * TILES, :] = jnp.where(d > x, both, 0.0).astype(BF16)
    both = split_sum(whole)
    for d in range(rows):
        send_ref[PACK * (d + 1) - 2 * TILES : PACK * (d + 1), :] = jnp.where(d > x, both, 0.0).astype(BF16)


def merge(place, got, rate, rows):
    return pl.pallas_call(
        merge_kernel,
        out_shape=(
            jax.ShapeDtypeStruct((rows * PACK, LANES), BF16),
            pltpu.VMEM((STATE * TILES, LANES), F32),
            pltpu.VMEM((TILES, LANES), F32),
        ),
        in_specs=[SMEM, VMEM, VMEM],
        out_specs=(VMEM,) * 3,
        compiler_params=params(8),
        name="merge",
    )(place, got, rate)


def finish_kernel(got_ref, state_ref, sum_ref, rate_ref, g_ref, y_ref, cum_ref, out_hbm, tot_ref, bc_ref, out_ref, sems):
    rows = out_hbm.shape[0]
    spread(g_ref[:, DT_RANK : DT_RANK + 2 * STATE].astype(F32), STATE, STATE, bc_ref)
    count = got_ref.shape[0] // PACK - 1
    sums = [sums_of(got_ref, k) for k in range(count)]
    incoming = []
    for n in range(0, STATE, 2):
        blocks = [states_of(got_ref, k, n) for k in range(count)]
        for h in range(2):
            rate = rate_ref[tile(n + h), :]
            run = blocks[0][tile(h)]
            for k in range(1, count):
                run = jnp.exp2(sums[k] * rate) * run + blocks[k][tile(h)]
            incoming.append(jnp.exp2(sum_ref[...] * rate) * run + state_ref[tile(n + h), :])

    def group(i, carry):
        t0 = pl.multiple_of(i * UNROLL, UNROLL)
        for r in range(UNROLL):
            t = t0 + r
            cum, y = cum_ref[token(t), :], y_ref[token(t), :]
            for n in range(STATE):
                read = jnp.broadcast_to(bc_ref[n, pl.ds(t, 1), :], cum.shape)
                y = y + jnp.exp2(cum * rate_ref[tile(n), :]) * (carry[n] * read)
            tot_ref[token(t), :] = y
        return carry

    pieces = sems.shape[0]
    some = rows // pieces

    def leave(i):
        at = pl.ds(pl.multiple_of(i * some, some), some)
        return pltpu.make_async_copy(out_ref.at[at], out_hbm.at[at], sems.at[i])

    def piece(i, carry):
        lax.fori_loop(i * (some // UNROLL), (i + 1) * (some // UNROLL), group, carry)
        at = pl.ds(pl.multiple_of(i * some, some), some)
        for j in range(TILES):
            rows_j = tot_ref[pl.ds(i * (some * TILES) + j, some, TILES), :]
            out_ref[at, LANES * j : LANES * (j + 1)] = rows_j.astype(BF16)
        leave(i).start()
        return carry

    lax.fori_loop(0, pieces, piece, tuple(incoming))
    for i in range(pieces):
        leave(i).wait()


def finish(got, states, sums, rate, g, y, cum):
    rows = g.shape[0]
    return pl.pallas_call(
        finish_kernel,
        out_shape=jax.ShapeDtypeStruct((rows, TILES * LANES), BF16),
        in_specs=[VMEM] * 7,
        out_specs=pl.BlockSpec(memory_space=pltpu.HBM),
        scratch_shapes=[
            pltpu.VMEM(y.shape, F32),
            pltpu.VMEM((STATE, rows, LANES), F32),
            pltpu.VMEM((rows, TILES * LANES), BF16),
            pltpu.SemaphoreType.DMA((4,)),
        ],
        compiler_params=params(8),
        name="finish",
    )(got, states, sums, rate, g, y, cum)


def shards(inputs, conv_weight, conv_bias, proj_weight, dt_weight, dt_bias, decay_rate, skip_gain):
    rows, width = inputs.shape
    seq, mp = lax.axis_size("seq"), lax.axis_size("mp")
    x_size, y_size = seq // Z, mp // 2
    on_z = [[Z * x + z for z in range(Z)] for x in range(x_size)]
    on_x = [[Z * x + z for x in range(x_size)] for z in range(Z)]
    on_y = [[2 * y + core for y in range(y_size)] for core in range(2)]
    on_chip = [[2 * y, 2 * y + 1] for y in range(y_size)]
    me = lax.axis_index("seq")
    place = jnp.stack([me % Z, me // Z, lax.axis_index("mp") % 2]).astype(jnp.int32)
    halo = lax.ppermute(inputs[rows - 8 :], "seq", [(s, s + 1) for s in range(seq - 1)])
    first, head, share, taps_in, bias, weight, dtw, dtb, rate, gain = mix(
        inputs,
        conv_weight,
        conv_bias.reshape(1, width),
        jnp.transpose(proj_weight),
        dt_weight,
        dt_bias.reshape(1, width),
        jnp.transpose(decay_rate),
        skip_gain.reshape(1, width),
    )
    mixed, ours, theirs = project(place, first, head, share, halo, taps_in, bias, weight)
    both = lax.all_gather(theirs, "mp", axis=0, tiled=True, axis_index_groups=on_chip)
    parts = lax.all_to_all(pair(place, ours, both), "mp", 0, 0, tiled=True, axis_index_groups=on_y)
    mine = lax.all_to_all(total(parts), "mp", 0, 0, tiled=True, axis_index_groups=on_y)
    projected = lax.all_gather(mine, "mp", axis=0, tiled=True, axis_index_groups=on_chip)
    dt, ends = state(projected, dtw, dtb, mixed, rate)
    got = lax.all_to_all(ends, "seq", 0, 0, tiled=True, axis_index_groups=on_z)
    y, cum, rate = local(projected, dt, rate, mixed, gain)
    ends, states, sums = merge(place, got, rate, x_size)
    got = lax.all_to_all(ends, "seq", 0, 0, tiled=True, axis_index_groups=on_x)
    return finish(got, states, sums, rate, projected, y, cum)


def solution(mesh):
    placed = (
        P("seq", "mp"),
        P(None, "mp"),
        P("mp"),
        P("mp", None),
        P(None, "mp"),
        P("mp"),
        P("mp", None),
        P("mp"),
    )
    return jax.shard_map(
        shards, mesh=mesh, in_specs=placed, out_specs=P("seq", "mp"), check_vma=False
    )
```

```python
import jax
import jax.numpy as jnp
from jax import lax
from jax.experimental import pallas as pl
from jax.experimental.pallas import tpu as pltpu
from jax.sharding import PartitionSpec as P

F32, BF16 = jnp.float32, jnp.bfloat16
STATE = 16
DT_RANK = 512
LANES, TILES = 128, 8
LOG2E = 1.4426950408889634
PACK = STATE * TILES + 2 * TILES
Z = 8
UNROLL = 16
VMEM = pl.BlockSpec(memory_space=pltpu.VMEM)
SMEM = pl.BlockSpec(memory_space=pltpu.SMEM)


def params(mib):
    return pltpu.CompilerParams(vmem_limit_bytes=mib << 20)


def cost(flops):
    return pl.CostEstimate(flops=flops, bytes_accessed=flops // 4, transcendentals=flops // 8)


def taps(pad_ref, w_ref, b_ref, first, count):
    pre = b_ref[...] + w_ref[0:1, :] * pad_ref[first + 5 : first + 5 + count, :]
    for k in range(1, 4):
        pre = pre + w_ref[k : k + 1, :] * pad_ref[first + 5 + k : first + 5 + k + count, :]
    return pre / (1.0 + jnp.exp(-pre))


def multiply(rows, weight_t):
    return lax.dot_general(rows, weight_t, (((1,), (1,)), ((), ())), preferred_element_type=F32).astype(BF16)


def mix_kernel(
    x_hbm, w_hbm, b_hbm, pw_hbm, dtw_hbm, dtb_hbm, decay_hbm, gain_hbm,
    mixed_ref, head_ref, share_ref, w_ref, b_ref, pw_ref, dtw_ref, dtb_ref, rate_ref, gain_ref,
    x_ref, pad_ref, decay_ref, row_ref, sems,
):
    rows = x_hbm.shape[0]
    step, parts = 16, 4
    some = rows // parts
    small = [
        pltpu.make_async_copy(source, target, sems.at[i])
        for i, (source, target) in enumerate(((w_hbm, w_ref), (b_hbm, b_ref)))
    ]
    chunks = [
        pltpu.make_async_copy(x_hbm.at[pl.ds(some * i, some)], x_ref.at[pl.ds(some * i, some)], sems.at[2 + i])
        for i in range(parts)
    ]
    later = [
        pltpu.make_async_copy(source, target, sems.at[2 + parts + i])
        for i, (source, target) in enumerate(
            ((decay_hbm, decay_ref), (gain_hbm, row_ref), (pw_hbm, pw_ref), (dtw_hbm, dtw_ref), (dtb_hbm, dtb_ref))
        )
    ]
    for copy in small + chunks + later:
        copy.start()
    pad_ref[0:8, :] = jnp.zeros_like(pad_ref[0:8, :])
    for copy in small:
        copy.wait()
    for i, copy in enumerate(chunks):
        copy.wait()
        for r in range(some * i, some * (i + 1), step):
            pad_ref[8 + r : 8 + r + step, :] = x_ref[r : r + step, :].astype(F32)
            mixed_ref[r : r + step, :] = taps(pad_ref, w_ref, b_ref, r, step).astype(BF16)
    head_ref[...] = pad_ref[8:16, :]
    for copy in later:
        copy.wait()
    for j in range(TILES):
        c = slice(LANES * j, LANES * (j + 1))
        rate_ref[pl.ds(j, STATE, TILES), :] = decay_ref[:, c] * -LOG2E
        gain_ref[j : j + 1, :] = row_ref[:, c]
    share_ref[...] = multiply(mixed_ref[...], pw_ref[...])


def mix(x, weight, bias, weight_t, dtw, dtb, decay, gain):
    rows, width = x.shape
    return pl.pallas_call(
        mix_kernel,
        out_shape=(
            pltpu.VMEM((rows, width), BF16),
            pltpu.VMEM((8, width), F32),
            pltpu.VMEM((rows, weight_t.shape[0]), BF16),
            pltpu.VMEM(weight.shape, F32),
            pltpu.VMEM(bias.shape, F32),
            pltpu.VMEM(weight_t.shape, BF16),
            pltpu.VMEM(dtw.shape, BF16),
            pltpu.VMEM(dtb.shape, F32),
            pltpu.VMEM((STATE * TILES, LANES), F32),
            pltpu.VMEM((TILES, LANES), F32),
        ),
        in_specs=[pl.BlockSpec(memory_space=pltpu.HBM)] * 8,
        out_specs=(VMEM,) * 10,
        scratch_shapes=[
            pltpu.VMEM((rows, width), BF16),
            pltpu.VMEM((rows + 8, width), F32),
            pltpu.VMEM(decay.shape, F32),
            pltpu.VMEM(gain.shape, F32),
            pltpu.SemaphoreType.DMA((11,)),
        ],
        compiler_params=params(60),
        cost_estimate=cost(20_000_000),
        name="mix",
    )(x, weight, bias, weight_t, dtw, dtb, decay, gain)


def project_kernel(
    place_ref, first_ref, head_ref, share_ref, halo_ref, w_ref, b_ref, pw_ref, mixed_ref, ours_ref, theirs_ref, pad_ref, all_ref
):
    pad_ref[0:8, :] = halo_ref[...].astype(F32)
    pad_ref[8:16, :] = head_ref[...]
    top = taps(pad_ref, w_ref, b_ref, 0, 8)
    top = jnp.concatenate([top, first_ref[0:16, :].astype(F32)[8:16]], axis=0).astype(BF16)
    mixed_ref[16:, :] = first_ref[16:, :]
    mixed_ref[0:16, :] = top
    all_ref[16:, :] = share_ref[16:, :]
    all_ref[0:16, :] = multiply(top, pw_ref[...])
    half = ours_ref.shape[0]
    core = place_ref[2]
    ours_ref[...] = all_ref[pl.ds(pl.multiple_of(core * half, half), half), :]
    theirs_ref[...] = all_ref[pl.ds(pl.multiple_of((1 - core) * half, half), half), :]


def project(place, first, head, share, halo, weight, bias, weight_t):
    rows, width = first.shape
    half = pltpu.VMEM((rows // 2, share.shape[1]), BF16)
    return pl.pallas_call(
        project_kernel,
        out_shape=(pltpu.VMEM((rows, width), BF16), half, half),
        in_specs=[SMEM] + [VMEM] * 7,
        out_specs=(VMEM,) * 3,
        scratch_shapes=[pltpu.VMEM((16, width), F32), pltpu.VMEM(share.shape, BF16)],
        compiler_params=params(8),
        name="project",
    )(place, first, head, share, halo, weight, bias, weight_t)


def pair_kernel(place_ref, ours_ref, got_ref, out_ref):
    half = out_ref.shape[0]
    theirs = pl.multiple_of((1 - place_ref[2]) * half, half)
    out_ref[...] = (ours_ref[...].astype(F32) + got_ref[pl.ds(theirs, half), :].astype(F32)).astype(BF16)


def pair(place, ours, got):
    return pl.pallas_call(
        pair_kernel,
        out_shape=jax.ShapeDtypeStruct(ours.shape, BF16),
        in_specs=[SMEM] + [VMEM] * 2,
        out_specs=VMEM,
        compiler_params=params(8),
        name="pair",
    )(place, ours, got)


def total_kernel(parts_ref, out_ref):
    rows = 16
    total = parts_ref[0:rows, :].astype(F32)
    for k in range(1, parts_ref.shape[0] // rows):
        total = total + parts_ref[rows * k : rows * (k + 1), :].astype(F32)
    for k in range(out_ref.shape[0] // rows):
        out_ref[rows * k : rows * (k + 1), :] = total.astype(BF16)


def total(parts):
    return pl.pallas_call(
        total_kernel,
        out_shape=jax.ShapeDtypeStruct(parts.shape, BF16),
        in_specs=[VMEM],
        out_specs=VMEM,
        compiler_params=params(8),
        name="total",
    )(parts)


def spread(columns, first, count, out_ref):
    for n in range(count):
        out_ref[n] = jnp.broadcast_to(
            columns[:, first + n : first + n + 1], (columns.shape[0], LANES)
        )


def tile(n):
    return slice(TILES * n, TILES * (n + 1))


def token(t):
    return pl.ds(pl.multiple_of(t * TILES, TILES), TILES)


def split_sum(value):
    high = value.astype(BF16).astype(F32)
    return jnp.concatenate([high, value - high], axis=0)


def sums_of(got_ref, k):
    both = got_ref[PACK * (k + 1) - 2 * TILES : PACK * (k + 1), :].astype(F32)
    return both[:TILES] + both[TILES:]


def states_of(got_ref, k, n):
    return got_ref[PACK * k + TILES * n : PACK * k + TILES * (n + 2), :].astype(F32)


def state_kernel(
    g_ref, dtw_ref, dtb_ref, mixed_ref, rate_ref, dt_hbm, send_ref, dt_ref, dx_ref, bc_ref, sem
):
    rows, width = mixed_ref.shape
    low = g_ref[:, 0:DT_RANK]
    for c in range(0, width, 256):
        pre = jnp.dot(low, dtw_ref[:, c : c + 256], preferred_element_type=F32)
        pre = pre + dtb_ref[:, c : c + 256]
        small = jnp.exp(-jnp.abs(pre))
        log1p = jnp.where(small < 1e-3, small - 0.5 * small * small, jnp.log(1.0 + small))
        dt = jnp.maximum(pre, 0.0) + log1p
        dx = dt * mixed_ref[:, c : c + 256].astype(F32)
        for h in range(2):
            at = pl.ds(c // LANES + h, rows, TILES)
            dt_ref[at, :] = dt[:, LANES * h : LANES * (h + 1)]
            dx_ref[at, :] = dx[:, LANES * h : LANES * (h + 1)]
    keep = pltpu.make_async_copy(dt_ref, dt_hbm, sem)
    keep.start()
    spread(g_ref[:, DT_RANK : DT_RANK + 2 * STATE].astype(F32), 0, STATE, bc_ref)

    def group(i, carry):
        states, total = list(carry[:STATE]), carry[STATE]
        t0 = pl.multiple_of(i * UNROLL, UNROLL)
        for r in range(UNROLL):
            dt, dx = dt_ref[token(t0 + r), :], dx_ref[token(t0 + r), :]
            total = total + dt
            for n in range(STATE):
                enter = jnp.broadcast_to(bc_ref[n, pl.ds(t0 + r, 1), :], dt.shape)
                states[n] = jnp.exp2(dt * rate_ref[tile(n), :]) * states[n] + dx * enter
        return (*states, total)

    zero = jnp.zeros((TILES, LANES), F32)
    final = lax.fori_loop(0, rows // UNROLL, group, (zero,) * (STATE + 1))
    pack = [jnp.concatenate(final[n : n + 2], axis=0).astype(BF16) for n in range(0, STATE, 2)]
    pack.append(split_sum(final[STATE]).astype(BF16))
    for k in range(send_ref.shape[0] // PACK):
        for i, piece in enumerate(pack):
            at = PACK * k + 2 * TILES * i
            send_ref[at : at + 2 * TILES, :] = piece
    keep.wait()


def state(g, dtw, dtb, mixed, rate):
    rows, width = mixed.shape
    return pl.pallas_call(
        state_kernel,
        out_shape=(
            pltpu.HBM((rows * TILES, LANES), F32),
            pltpu.VMEM((Z * PACK, LANES), BF16),
        ),
        in_specs=[VMEM] * 5,
        out_specs=(pl.BlockSpec(memory_space=pltpu.HBM), VMEM),
        scratch_shapes=[
            pltpu.VMEM((rows * TILES, LANES), F32),
            pltpu.VMEM((rows * TILES, LANES), F32),
            pltpu.VMEM((STATE, rows, LANES), F32),
            pltpu.SemaphoreType.DMA,
        ],
        compiler_params=params(12),
        name="state",
    )(g, dtw, dtb, mixed, rate)


def local_kernel(
    g_ref, dt_ref, rate_ref, mixed_ref, gain_ref, y_ref, e_hbm, rate_out, x_ref, bc_ref, e_ref, sems
):
    rows = mixed_ref.shape[0]
    chunk = e_ref.shape[1] // (STATE * TILES)
    rate_out[...] = rate_ref[...]
    spread(g_ref[:, DT_RANK : DT_RANK + 2 * STATE].astype(F32), 0, 2 * STATE, bc_ref)
    for j in range(TILES):
        x_ref[pl.ds(j, rows, TILES), :] = mixed_ref[:, LANES * j : LANES * (j + 1)].astype(F32)

    def leave(i, slot):
        size = chunk * STATE * TILES
        at = pl.ds(pl.multiple_of(i * size, size), size)
        return pltpu.make_async_copy(e_ref.at[slot], e_hbm.at[at], sems.at[slot])

    def group(first, slot):
        def one(i, carry):
            states, total = list(carry[:STATE]), carry[STATE]
            t0 = pl.multiple_of(i * UNROLL, UNROLL)
            for r in range(UNROLL):
                t = first + t0 + r
                dt, x = dt_ref[token(t), :], x_ref[token(t), :]
                dx, y = dt * x, gain_ref[...] * x
                total = total + dt
                weights = []
                for n in range(STATE):
                    enter = jnp.broadcast_to(bc_ref[n, pl.ds(t, 1), :], dt.shape)
                    read = jnp.broadcast_to(bc_ref[STATE + n, pl.ds(t, 1), :], dt.shape)
                    states[n] = jnp.exp2(dt * rate_ref[tile(n), :]) * states[n] + dx * enter
                    y = y + states[n] * read
                    weights.append(jnp.exp2(total * rate_ref[tile(n), :]) * read)
                    if n % 2:
                        at = (t0 + r) * (STATE * TILES) + TILES * (n - 1)
                        both = jnp.concatenate(weights[n - 1 :], axis=0).astype(BF16)
                        e_ref[slot, pl.ds(pl.multiple_of(at, 2 * TILES), 2 * TILES), :] = both
                y_ref[token(t), :] = y
            return (*states, total)

        return one

    def piece(i, carry):
        slot = lax.rem(i, 2)

        @pl.when(i >= 2)
        def _():
            leave(i - 2, slot).wait()

        carry = lax.fori_loop(0, chunk // UNROLL, group(pl.multiple_of(i * chunk, chunk), slot), carry)
        leave(i, slot).start()
        return carry

    zero = jnp.zeros((TILES, LANES), F32)
    pieces = rows // chunk
    lax.fori_loop(0, pieces, piece, (zero,) * (STATE + 1))
    for i in range(pieces - 2, pieces):
        leave(i, i % 2).wait()


def local(g, dt, rate, mixed, gain):
    rows = mixed.shape[0]
    flat = pltpu.VMEM((rows * TILES, LANES), F32)
    return pl.pallas_call(
        local_kernel,
        out_shape=(
            flat,
            pltpu.HBM((rows * STATE * TILES, LANES), BF16),
            pltpu.VMEM(rate.shape, F32),
        ),
        in_specs=[VMEM] * 5,
        out_specs=(VMEM, pl.BlockSpec(memory_space=pltpu.HBM), VMEM),
        scratch_shapes=[
            flat,
            pltpu.VMEM((2 * STATE, rows, LANES), F32),
            pltpu.VMEM((2, 32 * STATE * TILES, LANES), BF16),
            pltpu.SemaphoreType.DMA((2,)),
        ],
        compiler_params=params(12),
        cost_estimate=cost(60_000_000),
        name="local",
    )(g, dt, rate, mixed, gain)


def merge_kernel(place_ref, got_ref, rate_ref, send_ref, state_ref, sum_ref):
    rows, count = send_ref.shape[0] // PACK, got_ref.shape[0] // PACK
    z, x = place_ref[0], place_ref[1]
    zero = jnp.zeros((TILES, LANES), F32)
    sums = [sums_of(got_ref, k) for k in range(count)]
    whole, before = zero, zero
    for k in range(count):
        whole = whole + sums[k]
        before = before + jnp.where(k < z, sums[k], 0.0)
    sum_ref[...] = before
    for n in range(0, STATE, 2):
        blocks = [states_of(got_ref, k, n) for k in range(count)]
        ends, held = [], []
        for h in range(2):
            run, keep = zero, zero
            for k in range(count):
                keep = jnp.where(k == z, run, keep)
                run = jnp.exp2(sums[k] * rate_ref[tile(n + h), :]) * run + blocks[k][tile(h)]
            ends.append(run)
            held.append(keep)
        state_ref[TILES * n : TILES * (n + 2), :] = jnp.concatenate(held, axis=0)
        both = jnp.concatenate(ends, axis=0)
        for d in range(rows):
            at = PACK * d + TILES * n
            send_ref[at : at + 2 * TILES, :] = jnp.where(d > x, both, 0.0).astype(BF16)
    both = split_sum(whole)
    for d in range(rows):
        send_ref[PACK * (d + 1) - 2 * TILES : PACK * (d + 1), :] = jnp.where(d > x, both, 0.0).astype(BF16)


def merge(place, got, rate, rows):
    return pl.pallas_call(
        merge_kernel,
        out_shape=(
            jax.ShapeDtypeStruct((rows * PACK, LANES), BF16),
            pltpu.VMEM((STATE * TILES, LANES), F32),
            pltpu.VMEM((TILES, LANES), F32),
        ),
        in_specs=[SMEM, VMEM, VMEM],
        out_specs=(VMEM,) * 3,
        compiler_params=params(8),
        cost_estimate=cost(100_000_000),
        name="merge",
    )(place, got, rate)


def finish_kernel(got_ref, state_ref, sum_ref, rate_ref, y_ref, e_ref, out_hbm, tot_ref, out_ref, sems):
    rows = out_hbm.shape[0]
    count = got_ref.shape[0] // PACK - 1
    sums = [sums_of(got_ref, k) for k in range(count)]
    incoming = []
    for n in range(0, STATE, 2):
        blocks = [states_of(got_ref, k, n) for k in range(count)]
        for h in range(2):
            rate = rate_ref[tile(n + h), :]
            run = blocks[0][tile(h)]
            for k in range(1, count):
                run = jnp.exp2(sums[k] * rate) * run + blocks[k][tile(h)]
            incoming.append(jnp.exp2(sum_ref[...] * rate) * run + state_ref[tile(n + h), :])

    def group(i, carry):
        t0 = pl.multiple_of(i * UNROLL, UNROLL)
        for r in range(UNROLL):
            t = t0 + r
            more = []
            for n in range(0, STATE, 2):
                at = pl.multiple_of(t * STATE * TILES + n * TILES, 2 * TILES)
                both = e_ref[pl.ds(at, 2 * TILES), :].astype(F32)
                more.append(both[:TILES] * carry[n] + both[TILES:] * carry[n + 1])
            while len(more) > 1:
                more = [a + b for a, b in zip(more[::2], more[1::2])]
            tot_ref[token(t), :] = y_ref[token(t), :] + more[0]
        return carry

    pieces = sems.shape[0]
    some = rows // pieces

    def leave(i):
        at = pl.ds(pl.multiple_of(i * some, some), some)
        return pltpu.make_async_copy(out_ref.at[at], out_hbm.at[at], sems.at[i])

    def piece(i, carry):
        lax.fori_loop(i * (some // UNROLL), (i + 1) * (some // UNROLL), group, carry)
        at = pl.ds(pl.multiple_of(i * some, some), some)
        for j in range(TILES):
            rows_j = tot_ref[pl.ds(i * (some * TILES) + j, some, TILES), :]
            out_ref[at, LANES * j : LANES * (j + 1)] = rows_j.astype(BF16)
        leave(i).start()
        return carry

    lax.fori_loop(0, pieces, piece, tuple(incoming))
    for i in range(pieces):
        leave(i).wait()


def finish(got, states, sums, rate, y, e):
    rows = y.shape[0] // TILES
    return pl.pallas_call(
        finish_kernel,
        out_shape=jax.ShapeDtypeStruct((rows, TILES * LANES), BF16),
        in_specs=[VMEM] * 6,
        out_specs=pl.BlockSpec(memory_space=pltpu.HBM),
        scratch_shapes=[
            pltpu.VMEM(y.shape, F32),
            pltpu.VMEM((rows, TILES * LANES), BF16),
            pltpu.SemaphoreType.DMA((4,)),
        ],
        compiler_params=params(8),
        name="finish",
    )(got, states, sums, rate, y, e)


def shards(inputs, conv_weight, conv_bias, proj_weight, dt_weight, dt_bias, decay_rate, skip_gain):
    rows, width = inputs.shape
    seq, mp = lax.axis_size("seq"), lax.axis_size("mp")
    x_size, y_size = seq // Z, mp // 2
    on_z = [[Z * x + z for z in range(Z)] for x in range(x_size)]
    on_x = [[Z * x + z for x in range(x_size)] for z in range(Z)]
    on_y = [[2 * y + core for y in range(y_size)] for core in range(2)]
    on_chip = [[2 * y, 2 * y + 1] for y in range(y_size)]
    me = lax.axis_index("seq")
    place = jnp.stack([me % Z, me // Z, lax.axis_index("mp") % 2]).astype(jnp.int32)
    halo = lax.ppermute(inputs[rows - 8 :], "seq", [(s, s + 1) for s in range(seq - 1)])
    first, head, share, taps_in, bias, weight, dtw, dtb, rate, gain = mix(
        inputs,
        conv_weight,
        conv_bias.reshape(1, width),
        jnp.transpose(proj_weight),
        dt_weight,
        dt_bias.reshape(1, width),
        jnp.transpose(decay_rate),
        skip_gain.reshape(1, width),
    )
    mixed, ours, theirs = project(place, first, head, share, halo, taps_in, bias, weight)
    both = lax.all_gather(theirs, "mp", axis=0, tiled=True, axis_index_groups=on_chip)
    parts = lax.all_to_all(pair(place, ours, both), "mp", 0, 0, tiled=True, axis_index_groups=on_y)
    mine = lax.all_to_all(total(parts), "mp", 0, 0, tiled=True, axis_index_groups=on_y)
    projected = lax.all_gather(mine, "mp", axis=0, tiled=True, axis_index_groups=on_chip)
    dt, ends = state(projected, dtw, dtb, mixed, rate)
    got = lax.all_to_all(ends, "seq", 0, 0, tiled=True, axis_index_groups=on_z)
    y, e, rate = local(projected, dt, rate, mixed, gain)
    ends, states, sums = merge(place, got, rate, x_size)
    got = lax.all_to_all(ends, "seq", 0, 0, tiled=True, axis_index_groups=on_x)
    return finish(got, states, sums, rate, y, e)


def solution(mesh):
    placed = (
        P("seq", "mp"),
        P(None, "mp"),
        P("mp"),
        P("mp", None),
        P(None, "mp"),
        P("mp"),
        P("mp", None),
        P("mp"),
    )
    return jax.shard_map(
        shards, mesh=mesh, in_specs=placed, out_specs=P("seq", "mp"), check_vma=False
    )
```

```python
import jax
import jax.numpy as jnp
from jax import lax
from jax.experimental import pallas as pl
from jax.experimental.pallas import tpu as pltpu
from jax.sharding import PartitionSpec as P

F32, BF16 = jnp.float32, jnp.bfloat16
STATE = 16
DT_RANK = 512
LANES, TILES = 128, 8
LOG2E = 1.4426950408889634
PACK = STATE * TILES + 2 * TILES
Z = 8
UNROLL = 16
VMEM = pl.BlockSpec(memory_space=pltpu.VMEM)


def params(mib):
    return pltpu.CompilerParams(vmem_limit_bytes=mib << 20)


def cost(flops):
    return pl.CostEstimate(flops=flops, bytes_accessed=flops // 4, transcendentals=flops // 8)


def taps(pad_ref, w_ref, b_ref, first, count):
    pre = b_ref[...] + w_ref[0:1, :] * pad_ref[first + 5 : first + 5 + count, :]
    for k in range(1, 4):
        pre = pre + w_ref[k : k + 1, :] * pad_ref[first + 5 + k : first + 5 + k + count, :]
    return pre / (1.0 + jnp.exp(-pre))


def mix_kernel(
    x_hbm, w_hbm, b_hbm, pw_hbm, dtw_hbm, dtb_hbm, decay_hbm, gain_hbm,
    mixed_ref, head_ref, w_ref, b_ref, pw_ref, dtw_ref, dtb_ref, rate_ref, gain_ref,
    x_ref, pad_ref, decay_ref, row_ref, sems,
):
    rows = x_hbm.shape[0]
    step, parts = 16, 4
    some = rows // parts
    small = [
        pltpu.make_async_copy(source, target, sems.at[i])
        for i, (source, target) in enumerate(((w_hbm, w_ref), (b_hbm, b_ref)))
    ]
    chunks = [
        pltpu.make_async_copy(x_hbm.at[pl.ds(some * i, some)], x_ref.at[pl.ds(some * i, some)], sems.at[2 + i])
        for i in range(parts)
    ]
    later = [
        pltpu.make_async_copy(source, target, sems.at[2 + parts + i])
        for i, (source, target) in enumerate(
            ((decay_hbm, decay_ref), (gain_hbm, row_ref), (pw_hbm, pw_ref), (dtw_hbm, dtw_ref), (dtb_hbm, dtb_ref))
        )
    ]
    for copy in small + chunks + later:
        copy.start()
    pad_ref[0:8, :] = jnp.zeros_like(pad_ref[0:8, :])
    for copy in small:
        copy.wait()
    for i, copy in enumerate(chunks):
        copy.wait()
        for r in range(some * i, some * (i + 1), step):
            pad_ref[8 + r : 8 + r + step, :] = x_ref[r : r + step, :].astype(F32)
            mixed_ref[r : r + step, :] = taps(pad_ref, w_ref, b_ref, r, step).astype(BF16)
    head_ref[...] = pad_ref[8:16, :]
    for copy in later:
        copy.wait()
    for j in range(TILES):
        gain_ref[j : j + 1, :] = row_ref[:, lanes_of(j)]
    rate_ref[...] = decay_ref[...] * -LOG2E


def mix(x, weight, bias, weight_t, dtw, dtb, decay, gain):
    rows, width = x.shape
    return pl.pallas_call(
        mix_kernel,
        out_shape=(
            pltpu.VMEM((rows, width), BF16),
            pltpu.VMEM((8, width), F32),
            pltpu.VMEM(weight.shape, F32),
            pltpu.VMEM(bias.shape, F32),
            pltpu.VMEM(weight_t.shape, BF16),
            pltpu.VMEM(dtw.shape, BF16),
            pltpu.VMEM(dtb.shape, F32),
            pltpu.VMEM(decay.shape, F32),
            pltpu.VMEM((TILES, LANES), F32),
        ),
        in_specs=[pl.BlockSpec(memory_space=pltpu.HBM)] * 8,
        out_specs=(VMEM,) * 9,
        scratch_shapes=[
            pltpu.VMEM((rows, width), BF16),
            pltpu.VMEM((rows + 8, width), F32),
            pltpu.VMEM(decay.shape, F32),
            pltpu.VMEM(gain.shape, F32),
            pltpu.SemaphoreType.DMA((11,)),
        ],
        compiler_params=params(60),
        cost_estimate=cost(20_000_000),
        name="mix",
    )(x, weight, bias, weight_t, dtw, dtb, decay, gain)


def project_kernel(
    mixed_in, head_ref, halo_ref, w_ref, b_ref, pw_ref, mixed_ref, share_ref, theirs_ref, pad_ref
):
    pad_ref[0:8, :] = halo_ref[...].astype(F32)
    pad_ref[8:16, :] = head_ref[...]
    top = taps(pad_ref, w_ref, b_ref, 0, 8)
    mixed_ref[16:, :] = mixed_in[16:, :]
    mixed_ref[0:16, :] = jnp.concatenate([top, mixed_in[0:16, :].astype(F32)[8:16]], axis=0).astype(BF16)
    share_ref[...] = lax.dot_general(
        mixed_ref[...], pw_ref[...], (((1,), (1,)), ((), ())), preferred_element_type=F32
    ).astype(BF16)
    half = theirs_ref.shape[0]
    core = lax.rem(lax.axis_index("mp"), 2)
    theirs_ref[...] = share_ref[pl.ds(pl.multiple_of((1 - core) * half, half), half), :]


def project(mixed, head, halo, weight, bias, weight_t):
    rows, width = mixed.shape
    columns = weight_t.shape[0]
    return pl.pallas_call(
        project_kernel,
        out_shape=(
            pltpu.VMEM((rows, width), BF16),
            pltpu.VMEM((rows, columns), BF16),
            pltpu.VMEM((rows // 2, columns), BF16),
        ),
        in_specs=[VMEM] * 6,
        out_specs=(VMEM,) * 3,
        scratch_shapes=[pltpu.VMEM((16, width), F32)],
        compiler_params=params(8),
        name="project",
    )(mixed, head, halo, weight, bias, weight_t)


def pair_kernel(share_ref, got_ref, out_ref):
    half = out_ref.shape[0]
    core = lax.rem(lax.axis_index("mp"), 2)
    ours = share_ref[pl.ds(pl.multiple_of(core * half, half), half), :]
    theirs = got_ref[pl.ds(pl.multiple_of((1 - core) * half, half), half), :]
    out_ref[...] = (ours.astype(F32) + theirs.astype(F32)).astype(BF16)


def pair(share, got):
    return pl.pallas_call(
        pair_kernel,
        out_shape=jax.ShapeDtypeStruct((share.shape[0] // 2, share.shape[1]), BF16),
        in_specs=[VMEM] * 2,
        out_specs=VMEM,
        compiler_params=params(8),
        name="pair",
    )(share, got)


def total_kernel(parts_ref, out_ref):
    rows = 16
    total = parts_ref[0:rows, :].astype(F32)
    for k in range(1, parts_ref.shape[0] // rows):
        total = total + parts_ref[rows * k : rows * (k + 1), :].astype(F32)
    for k in range(out_ref.shape[0] // rows):
        out_ref[rows * k : rows * (k + 1), :] = total.astype(BF16)


def total(parts):
    return pl.pallas_call(
        total_kernel,
        out_shape=jax.ShapeDtypeStruct(parts.shape, BF16),
        in_specs=[VMEM],
        out_specs=VMEM,
        compiler_params=params(8),
        name="total",
    )(parts)


def spread(columns, first, count, out_ref):
    for n in range(count):
        out_ref[n] = jnp.broadcast_to(
            columns[:, first + n : first + n + 1], (columns.shape[0], LANES)
        )


def lanes_of(j):
    return slice(LANES * j, LANES * (j + 1))


def tile(n):
    return slice(TILES * n, TILES * (n + 1))


def token(t):
    return pl.ds(pl.multiple_of(t * TILES, TILES), TILES)


def send_sums(row_ref, send_ref, at, keep=None):
    value = row_ref[...]
    high = value.astype(BF16).astype(F32)
    both = jnp.concatenate([high, value - high], axis=0)
    if keep is not None:
        both = jnp.where(keep, both, 0.0)
    send_ref[at : at + 2 * TILES, :] = both.astype(BF16)


def state_kernel(
    g_ref, dtw_ref, dtb_ref, mixed_ref, rate_ref, dt_hbm, send_ref, dt_ref, enter_ref, sum_ref, sems
):
    rows, width = mixed_ref.shape
    low = g_ref[:, 0:DT_RANK]
    enter = jnp.transpose(g_ref[:, DT_RANK : DT_RANK + 2 * STATE].astype(F32))[:STATE]
    row = lax.broadcasted_iota(jnp.int32, enter.shape, 0)
    for n in range(STATE):
        enter_ref[STATE * n : STATE * (n + 1), :] = jnp.where(row == n, enter, 0.0).astype(BF16)
    here = lax.broadcasted_iota(jnp.int32, (rows, rows), 0)
    there = lax.broadcasted_iota(jnp.int32, (rows, rows), 1)
    later = (there > here).astype(F32).astype(BF16)
    copies = []
    for i, c in enumerate(range(0, width, 256)):
        at = slice(c, c + 256)
        pre = jnp.dot(low, dtw_ref[:, at], preferred_element_type=F32) + dtb_ref[:, at]
        small = jnp.exp(-jnp.abs(pre))
        log1p = jnp.where(small < 1e-3, small - 0.5 * small * small, jnp.log(1.0 + small))
        dt = jnp.maximum(pre, 0.0) + log1p
        dt_ref[:, at] = dt
        copies.append(pltpu.make_async_copy(dt_ref.at[:, at], dt_hbm.at[:, at], sems.at[i]))
        copies[-1].start()
        dx = dt * mixed_ref[:, at].astype(F32)
        rem = jnp.dot(later, dt.astype(BF16), preferred_element_type=F32)
        whole = jnp.sum(dt, axis=0, keepdims=True)
        ends = jnp.zeros((STATE, 256), F32)
        for n in range(STATE):
            part = (jnp.exp2(rem * rate_ref[n : n + 1, at]) * dx).astype(BF16)
            ends = ends + jnp.dot(enter_ref[STATE * n : STATE * (n + 1), :], part, preferred_element_type=F32)
        for h in range(2):
            j = c // LANES + h
            sum_ref[j : j + 1, :] = whole[:, lanes_of(h)]
            for k in range(Z):
                send_ref[PACK * k + STATE * j : PACK * k + STATE * (j + 1), :] = ends[:, lanes_of(h)].astype(BF16)
    for k in range(Z):
        send_sums(sum_ref, send_ref, PACK * k + STATE * TILES)
    for copy in copies:
        copy.wait()


def state(g, dtw, dtb, mixed, rate):
    rows, width = mixed.shape
    return pl.pallas_call(
        state_kernel,
        out_shape=(
            pltpu.HBM((rows, width), F32),
            pltpu.VMEM((Z * PACK, LANES), BF16),
        ),
        in_specs=[VMEM] * 5,
        out_specs=(pl.BlockSpec(memory_space=pltpu.HBM), VMEM),
        scratch_shapes=[
            pltpu.VMEM((rows, width), F32),
            pltpu.VMEM((STATE * STATE, rows), BF16),
            pltpu.VMEM((TILES, LANES), F32),
            pltpu.SemaphoreType.DMA((width // 256,)),
        ],
        compiler_params=params(12),
        name="state",
    )(g, dtw, dtb, mixed, rate)


def local_kernel(
    g_ref, step_ref, decay_ref, mixed_ref, gain_ref, y_ref, e_hbm, rate_out, x_ref, dt_ref, rate_ref, bc_ref, e_ref, sems
):
    rows = mixed_ref.shape[0]
    chunk = e_ref.shape[1] // (STATE * TILES)
    rate_out[...] = decay_ref[...]
    spread(g_ref[:, DT_RANK : DT_RANK + 2 * STATE].astype(F32), 0, 2 * STATE, bc_ref)
    for j in range(TILES):
        x_ref[pl.ds(j, rows, TILES), :] = mixed_ref[:, lanes_of(j)].astype(F32)
        dt_ref[pl.ds(j, rows, TILES), :] = step_ref[:, lanes_of(j)]
        rate_ref[pl.ds(j, STATE, TILES), :] = decay_ref[:, lanes_of(j)]

    def leave(i, slot):
        size = chunk * STATE * TILES
        at = pl.ds(pl.multiple_of(i * size, size), size)
        return pltpu.make_async_copy(e_ref.at[slot], e_hbm.at[at], sems.at[slot])

    def group(first, slot):
        def one(i, carry):
            states, total = list(carry[:STATE]), carry[STATE]
            t0 = pl.multiple_of(i * UNROLL, UNROLL)
            for r in range(UNROLL):
                t = first + t0 + r
                dt, x = dt_ref[token(t), :], x_ref[token(t), :]
                dx, y = dt * x, gain_ref[...] * x
                total = total + dt
                weights = []
                for n in range(STATE):
                    enter = jnp.broadcast_to(bc_ref[n, pl.ds(t, 1), :], dt.shape)
                    read = jnp.broadcast_to(bc_ref[STATE + n, pl.ds(t, 1), :], dt.shape)
                    states[n] = jnp.exp2(dt * rate_ref[tile(n), :]) * states[n] + dx * enter
                    y = y + states[n] * read
                    weights.append(jnp.exp2(total * rate_ref[tile(n), :]) * read)
                    if n % 2:
                        at = (t0 + r) * (STATE * TILES) + TILES * (n - 1)
                        both = jnp.concatenate(weights[n - 1 :], axis=0).astype(BF16)
                        e_ref[slot, pl.ds(pl.multiple_of(at, 2 * TILES), 2 * TILES), :] = both
                y_ref[token(t), :] = y
            return (*states, total)

        return one

    def piece(i, carry):
        slot = lax.rem(i, 2)

        @pl.when(i >= 2)
        def _():
            leave(i - 2, slot).wait()

        carry = lax.fori_loop(0, chunk // UNROLL, group(pl.multiple_of(i * chunk, chunk), slot), carry)
        leave(i, slot).start()
        return carry

    zero = jnp.zeros((TILES, LANES), F32)
    pieces = rows // chunk
    lax.fori_loop(0, pieces, piece, (zero,) * (STATE + 1))
    for i in range(pieces - 2, pieces):
        leave(i, i % 2).wait()


def local(g, dt, rate, mixed, gain):
    rows = mixed.shape[0]
    flat = pltpu.VMEM((rows * TILES, LANES), F32)
    return pl.pallas_call(
        local_kernel,
        out_shape=(
            flat,
            pltpu.HBM((rows * STATE * TILES, LANES), BF16),
            pltpu.VMEM(rate.shape, F32),
        ),
        in_specs=[VMEM] * 5,
        out_specs=(VMEM, pl.BlockSpec(memory_space=pltpu.HBM), VMEM),
        scratch_shapes=[
            flat,
            flat,
            pltpu.VMEM((STATE * TILES, LANES), F32),
            pltpu.VMEM((2 * STATE, rows, LANES), F32),
            pltpu.VMEM((2, 32 * STATE * TILES, LANES), BF16),
            pltpu.SemaphoreType.DMA((2,)),
        ],
        compiler_params=params(12),
        cost_estimate=cost(60_000_000),
        name="local",
    )(g, dt, rate, mixed, gain)


def unpack_sums(got_ref, count, sum_ref):
    for k in range(count):
        both = got_ref[PACK * (k + 1) - 2 * TILES : PACK * (k + 1), :].astype(F32)
        sum_ref[TILES * k : TILES * (k + 1), :] = both[:TILES] + both[TILES:]


def hand_on(got_ref, sum_ref, rate, k, j, run):
    end = got_ref[PACK * k + STATE * j : PACK * k + STATE * (j + 1), :].astype(F32)
    steps = jnp.broadcast_to(sum_ref[TILES * k + j : TILES * k + j + 1, :], end.shape)
    return jnp.exp2(steps * rate) * run + end


def merge_kernel(got_ref, rate_ref, send_ref, state_ref, before_ref, sum_ref, whole_ref):
    rows, count = send_ref.shape[0] // PACK, got_ref.shape[0] // PACK
    me = lax.axis_index("seq")
    z, x = lax.rem(me, Z), me // Z
    unpack_sums(got_ref, count, sum_ref)
    whole = before = jnp.zeros((TILES, LANES), F32)
    for k in range(count):
        steps = sum_ref[TILES * k : TILES * (k + 1), :]
        whole = whole + steps
        before = before + jnp.where(k < z, steps, 0.0)
    before_ref[...] = before
    whole_ref[...] = whole
    for j in range(TILES):
        rate = rate_ref[:, lanes_of(j)]
        run = kept = jnp.zeros((STATE, LANES), F32)
        for k in range(count):
            kept = jnp.where(k == z, run, kept)
            run = hand_on(got_ref, sum_ref, rate, k, j, run)
        state_ref[STATE * j : STATE * (j + 1), :] = kept
        for d in range(rows):
            send_ref[PACK * d + STATE * j : PACK * d + STATE * (j + 1), :] = jnp.where(d > x, run, 0.0).astype(BF16)
    for d in range(rows):
        send_sums(whole_ref, send_ref, PACK * d + STATE * TILES, d > x)


def merge(got, rate, rows):
    return pl.pallas_call(
        merge_kernel,
        out_shape=(
            jax.ShapeDtypeStruct((rows * PACK, LANES), BF16),
            pltpu.VMEM((STATE * TILES, LANES), F32),
            pltpu.VMEM((TILES, LANES), F32),
        ),
        in_specs=[VMEM, VMEM],
        out_specs=(VMEM,) * 3,
        scratch_shapes=[pltpu.VMEM((Z * TILES, LANES), F32), pltpu.VMEM((TILES, LANES), F32)],
        compiler_params=params(8),
        cost_estimate=cost(100_000_000),
        name="merge",
    )(got, rate)


def finish_kernel(
    got_ref, state_ref, before_ref, rate_ref, y_ref, e_ref, out_hbm, tot_ref, out_ref, sum_ref, in_ref, sems
):
    rows = out_hbm.shape[0]
    count = got_ref.shape[0] // PACK - 1
    unpack_sums(got_ref, count, sum_ref)
    for j in range(TILES):
        rate = rate_ref[:, lanes_of(j)]
        run = jnp.zeros((STATE, LANES), F32)
        for k in range(count):
            run = hand_on(got_ref, sum_ref, rate, k, j, run)
        steps = jnp.broadcast_to(before_ref[j : j + 1, :], run.shape)
        at = slice(STATE * j, STATE * (j + 1))
        in_ref[at, :] = jnp.exp2(steps * rate) * run + state_ref[at, :]
    incoming = [in_ref[pl.ds(n, TILES, STATE), :] for n in range(STATE)]

    def group(i, carry):
        t0 = pl.multiple_of(i * UNROLL, UNROLL)
        for r in range(UNROLL):
            t = t0 + r
            more = []
            for n in range(0, STATE, 2):
                at = pl.multiple_of(t * STATE * TILES + n * TILES, 2 * TILES)
                both = e_ref[pl.ds(at, 2 * TILES), :].astype(F32)
                more.append(both[:TILES] * carry[n] + both[TILES:] * carry[n + 1])
            while len(more) > 1:
                more = [a + b for a, b in zip(more[::2], more[1::2])]
            tot_ref[token(t), :] = y_ref[token(t), :] + more[0]
        return carry

    pieces = sems.shape[0]
    some = rows // pieces

    def leave(i):
        at = pl.ds(pl.multiple_of(i * some, some), some)
        return pltpu.make_async_copy(out_ref.at[at], out_hbm.at[at], sems.at[i])

    def piece(i, carry):
        lax.fori_loop(i * (some // UNROLL), (i + 1) * (some // UNROLL), group, carry)
        at = pl.ds(pl.multiple_of(i * some, some), some)
        for j in range(TILES):
            rows_j = tot_ref[pl.ds(i * (some * TILES) + j, some, TILES), :]
            out_ref[at, LANES * j : LANES * (j + 1)] = rows_j.astype(BF16)
        leave(i).start()
        return carry

    lax.fori_loop(0, pieces, piece, tuple(incoming))
    for i in range(pieces):
        leave(i).wait()


def finish(got, states, sums, rate, y, e):
    rows = y.shape[0] // TILES
    return pl.pallas_call(
        finish_kernel,
        out_shape=jax.ShapeDtypeStruct((rows, TILES * LANES), BF16),
        in_specs=[VMEM] * 6,
        out_specs=pl.BlockSpec(memory_space=pltpu.HBM),
        scratch_shapes=[
            pltpu.VMEM(y.shape, F32),
            pltpu.VMEM((rows, TILES * LANES), BF16),
            pltpu.VMEM((Z * TILES, LANES), F32),
            pltpu.VMEM((STATE * TILES, LANES), F32),
            pltpu.SemaphoreType.DMA((4,)),
        ],
        compiler_params=params(8),
        name="finish",
    )(got, states, sums, rate, y, e)


def shards(inputs, conv_weight, conv_bias, proj_weight, dt_weight, dt_bias, decay_rate, skip_gain):
    rows, width = inputs.shape
    seq, mp = lax.axis_size("seq"), lax.axis_size("mp")
    x_size, y_size = seq // Z, mp // 2
    on_z = [[Z * x + z for z in range(Z)] for x in range(x_size)]
    on_x = [[Z * x + z for x in range(x_size)] for z in range(Z)]
    on_y = [[2 * y + core for y in range(y_size)] for core in range(2)]
    on_chip = [[2 * y, 2 * y + 1] for y in range(y_size)]

    halo = lax.ppermute(inputs[rows - 8 :], "seq", [(s, s + 1) for s in range(seq - 1)])
    mixed, head, taps_in, bias, weight, dtw, dtb, rate, gain = mix(
        inputs,
        conv_weight,
        conv_bias.reshape(1, width),
        jnp.transpose(proj_weight),
        dt_weight,
        dt_bias.reshape(1, width),
        jnp.transpose(decay_rate),
        skip_gain.reshape(1, width),
    )
    mixed, share, theirs = project(mixed, head, halo, taps_in, bias, weight)
    both = lax.all_gather(theirs, "mp", axis=0, tiled=True, axis_index_groups=on_chip)
    parts = lax.all_to_all(pair(share, both), "mp", 0, 0, tiled=True, axis_index_groups=on_y)
    mine = lax.all_to_all(total(parts), "mp", 0, 0, tiled=True, axis_index_groups=on_y)
    projected = lax.all_gather(mine, "mp", axis=0, tiled=True, axis_index_groups=on_chip)
    dt, ends = state(projected, dtw, dtb, mixed, rate)
    got = lax.all_to_all(ends, "seq", 0, 0, tiled=True, axis_index_groups=on_z)
    y, e, rate = local(projected, dt, rate, mixed, gain)
    ends, states, sums = merge(got, rate, x_size)
    got = lax.all_to_all(ends, "seq", 0, 0, tiled=True, axis_index_groups=on_x)
    return finish(got, states, sums, rate, y, e)


def solution(mesh):
    placed = (
        P("seq", "mp"),
        P(None, "mp"),
        P("mp"),
        P("mp", None),
        P(None, "mp"),
        P("mp"),
        P("mp", None),
        P("mp"),
    )
    return jax.shard_map(
        shards, mesh=mesh, in_specs=placed, out_specs=P("seq", "mp"), check_vma=False
    )
```

```python
import jax
import jax.numpy as jnp
from jax import lax
from jax.experimental import pallas as pl
from jax.experimental.pallas import tpu as pltpu
from jax.sharding import PartitionSpec as P

F32, BF16 = jnp.float32, jnp.bfloat16
STATE = 16
DT_RANK = 512
LANES, TILES = 128, 8
LOG2E = 1.4426950408889634
PACK = STATE * TILES + 2 * TILES
Z = 8
UNROLL = 16
VMEM = pl.BlockSpec(memory_space=pltpu.VMEM)


def params(mib):
    return pltpu.CompilerParams(vmem_limit_bytes=mib << 20)


def cost(flops):
    return pl.CostEstimate(flops=flops, bytes_accessed=flops // 4, transcendentals=flops // 8)


def taps(pad_ref, w_ref, b_ref, first, count):
    pre = b_ref[...] + w_ref[0:1, :] * pad_ref[first + 5 : first + 5 + count, :]
    for k in range(1, 4):
        pre = pre + w_ref[k : k + 1, :] * pad_ref[first + 5 + k : first + 5 + k + count, :]
    return pre / (1.0 + jnp.exp(-pre))


def mix_kernel(
    x_hbm, w_hbm, b_hbm, pw_hbm, dtw_hbm, dtb_hbm, decay_hbm, gain_hbm,
    mixed_ref, head_ref, w_ref, b_ref, pw_ref, dtw_ref, dtb_ref, rate_ref, gain_ref,
    x_ref, pad_ref, decay_ref, row_ref, sems,
):
    rows = x_hbm.shape[0]
    step, parts = 16, 4
    some = rows // parts
    small = [
        pltpu.make_async_copy(source, target, sems.at[i])
        for i, (source, target) in enumerate(((w_hbm, w_ref), (b_hbm, b_ref)))
    ]
    chunks = [
        pltpu.make_async_copy(x_hbm.at[pl.ds(some * i, some)], x_ref.at[pl.ds(some * i, some)], sems.at[2 + i])
        for i in range(parts)
    ]
    later = [
        pltpu.make_async_copy(source, target, sems.at[2 + parts + i])
        for i, (source, target) in enumerate(
            ((decay_hbm, decay_ref), (gain_hbm, row_ref), (pw_hbm, pw_ref), (dtw_hbm, dtw_ref), (dtb_hbm, dtb_ref))
        )
    ]
    for copy in small + chunks + later:
        copy.start()
    pad_ref[0:8, :] = jnp.zeros_like(pad_ref[0:8, :])
    for copy in small:
        copy.wait()
    for i, copy in enumerate(chunks):
        copy.wait()
        for r in range(some * i, some * (i + 1), step):
            pad_ref[8 + r : 8 + r + step, :] = x_ref[r : r + step, :].astype(F32)
            mixed_ref[r : r + step, :] = taps(pad_ref, w_ref, b_ref, r, step).astype(BF16)
    head_ref[...] = pad_ref[8:16, :]
    for copy in later:
        copy.wait()
    for j in range(TILES):
        gain_ref[j : j + 1, :] = row_ref[:, lanes_of(j)]
    rate_ref[...] = decay_ref[...] * -LOG2E


def mix(x, weight, bias, weight_t, dtw, dtb, decay, gain):
    rows, width = x.shape
    return pl.pallas_call(
        mix_kernel,
        out_shape=(
            pltpu.VMEM((rows, width), BF16),
            pltpu.VMEM((8, width), F32),
            pltpu.VMEM(weight.shape, F32),
            pltpu.VMEM(bias.shape, F32),
            pltpu.VMEM(weight_t.shape, BF16),
            pltpu.VMEM(dtw.shape, BF16),
            pltpu.VMEM(dtb.shape, F32),
            pltpu.VMEM(decay.shape, F32),
            pltpu.VMEM((TILES, LANES), F32),
        ),
        in_specs=[pl.BlockSpec(memory_space=pltpu.HBM)] * 8,
        out_specs=(VMEM,) * 9,
        scratch_shapes=[
            pltpu.VMEM((rows, width), BF16),
            pltpu.VMEM((rows + 8, width), F32),
            pltpu.VMEM(decay.shape, F32),
            pltpu.VMEM(gain.shape, F32),
            pltpu.SemaphoreType.DMA((11,)),
        ],
        compiler_params=params(60),
        cost_estimate=cost(20_000_000),
        name="mix",
    )(x, weight, bias, weight_t, dtw, dtb, decay, gain)


def project_kernel(
    mixed_in, head_ref, halo_ref, w_ref, b_ref, pw_ref, mixed_ref, share_ref, theirs_ref, pad_ref
):
    pad_ref[0:8, :] = halo_ref[...].astype(F32)
    pad_ref[8:16, :] = head_ref[...]
    top = taps(pad_ref, w_ref, b_ref, 0, 8)
    mixed_ref[16:, :] = mixed_in[16:, :]
    mixed_ref[0:16, :] = jnp.concatenate([top, mixed_in[0:16, :].astype(F32)[8:16]], axis=0).astype(BF16)
    share_ref[...] = lax.dot_general(
        mixed_ref[...], pw_ref[...], (((1,), (1,)), ((), ())), preferred_element_type=F32
    ).astype(BF16)
    half = theirs_ref.shape[0]
    core = lax.rem(lax.axis_index("mp"), 2)
    theirs_ref[...] = share_ref[pl.ds(pl.multiple_of((1 - core) * half, half), half), :]


def project(mixed, head, halo, weight, bias, weight_t):
    rows, width = mixed.shape
    columns = weight_t.shape[0]
    return pl.pallas_call(
        project_kernel,
        out_shape=(
            pltpu.VMEM((rows, width), BF16),
            pltpu.VMEM((rows, columns), BF16),
            pltpu.VMEM((rows // 2, columns), BF16),
        ),
        in_specs=[VMEM] * 6,
        out_specs=(VMEM,) * 3,
        scratch_shapes=[pltpu.VMEM((16, width), F32)],
        compiler_params=params(8),
        name="project",
    )(mixed, head, halo, weight, bias, weight_t)


def pair_kernel(share_ref, got_ref, out_ref):
    half = out_ref.shape[0]
    core = lax.rem(lax.axis_index("mp"), 2)
    ours = share_ref[pl.ds(pl.multiple_of(core * half, half), half), :]
    theirs = got_ref[pl.ds(pl.multiple_of((1 - core) * half, half), half), :]
    out_ref[...] = (ours.astype(F32) + theirs.astype(F32)).astype(BF16)


def pair(share, got):
    return pl.pallas_call(
        pair_kernel,
        out_shape=jax.ShapeDtypeStruct((share.shape[0] // 2, share.shape[1]), BF16),
        in_specs=[VMEM] * 2,
        out_specs=VMEM,
        compiler_params=params(8),
        name="pair",
    )(share, got)


def total_kernel(parts_ref, out_ref):
    rows = 16
    total = parts_ref[0:rows, :].astype(F32)
    for k in range(1, parts_ref.shape[0] // rows):
        total = total + parts_ref[rows * k : rows * (k + 1), :].astype(F32)
    for k in range(out_ref.shape[0] // rows):
        out_ref[rows * k : rows * (k + 1), :] = total.astype(BF16)


def total(parts):
    return pl.pallas_call(
        total_kernel,
        out_shape=jax.ShapeDtypeStruct(parts.shape, BF16),
        in_specs=[VMEM],
        out_specs=VMEM,
        compiler_params=params(8),
        name="total",
    )(parts)


def spread(columns, first, count, out_ref):
    for n in range(count):
        out_ref[n] = jnp.broadcast_to(
            columns[:, first + n : first + n + 1], (columns.shape[0], LANES)
        )


def lanes_of(j):
    return slice(LANES * j, LANES * (j + 1))


def tile(n):
    return slice(TILES * n, TILES * (n + 1))


def token(t):
    return pl.ds(pl.multiple_of(t * TILES, TILES), TILES)


def send_sums(row_ref, send_ref, at, keep=None):
    value = row_ref[...]
    high = value.astype(BF16).astype(F32)
    both = jnp.concatenate([high, value - high], axis=0)
    if keep is not None:
        both = jnp.where(keep, both, 0.0)
    send_ref[at : at + 2 * TILES, :] = both.astype(BF16)


def state_kernel(
    g_ref, dtw_ref, dtb_ref, mixed_ref, rate_ref, dt_hbm, send_ref, dt_ref, enter_ref, sum_ref, sems
):
    rows, width = mixed_ref.shape
    low = g_ref[:, 0:DT_RANK]
    enter = jnp.transpose(g_ref[:, DT_RANK : DT_RANK + 2 * STATE].astype(F32))[:STATE]
    row = lax.broadcasted_iota(jnp.int32, enter.shape, 0)
    for n in range(STATE):
        enter_ref[STATE * n : STATE * (n + 1), :] = jnp.where(row == n, enter, 0.0).astype(BF16)
    here = lax.broadcasted_iota(jnp.int32, (rows, rows), 0)
    there = lax.broadcasted_iota(jnp.int32, (rows, rows), 1)
    later = (there > here).astype(F32).astype(BF16)
    copies = []
    for i, c in enumerate(range(0, width, 256)):
        at = slice(c, c + 256)
        pre = jnp.dot(low, dtw_ref[:, at], preferred_element_type=F32) + dtb_ref[:, at]
        small = jnp.exp(-jnp.abs(pre))
        log1p = jnp.where(small < 1e-3, small - 0.5 * small * small, jnp.log(1.0 + small))
        dt = jnp.maximum(pre, 0.0) + log1p
        dt_ref[:, at] = dt
        copies.append(pltpu.make_async_copy(dt_ref.at[:, at], dt_hbm.at[:, at], sems.at[i]))
        copies[-1].start()
        dx = dt * mixed_ref[:, at].astype(F32)
        rem = jnp.dot(later, dt.astype(BF16), preferred_element_type=F32)
        whole = jnp.sum(dt, axis=0, keepdims=True)
        ends = jnp.zeros((STATE, 256), F32)
        for n in range(STATE):
            part = (jnp.exp2(rem * rate_ref[n : n + 1, at]) * dx).astype(BF16)
            ends = ends + jnp.dot(enter_ref[STATE * n : STATE * (n + 1), :], part, preferred_element_type=F32)
        for h in range(2):
            j = c // LANES + h
            sum_ref[j : j + 1, :] = whole[:, lanes_of(h)]
            for k in range(Z):
                send_ref[PACK * k + STATE * j : PACK * k + STATE * (j + 1), :] = ends[:, lanes_of(h)].astype(BF16)
    for k in range(Z):
        send_sums(sum_ref, send_ref, PACK * k + STATE * TILES)
    for copy in copies:
        copy.wait()


def state(g, dtw, dtb, mixed, rate):
    rows, width = mixed.shape
    return pl.pallas_call(
        state_kernel,
        out_shape=(
            pltpu.HBM((rows, width), F32),
            pltpu.VMEM((Z * PACK, LANES), BF16),
        ),
        in_specs=[VMEM] * 5,
        out_specs=(pl.BlockSpec(memory_space=pltpu.HBM), VMEM),
        scratch_shapes=[
            pltpu.VMEM((rows, width), F32),
            pltpu.VMEM((STATE * STATE, rows), BF16),
            pltpu.VMEM((TILES, LANES), F32),
            pltpu.SemaphoreType.DMA((width // 256,)),
        ],
        compiler_params=params(12),
        name="state",
    )(g, dtw, dtb, mixed, rate)


def local_kernel(
    g_ref, step_ref, decay_ref, mixed_ref, gain_ref, y_ref, e_hbm, rate_out, x_ref, dt_ref, rate_ref, bc_ref, e_ref, sems
):
    rows = mixed_ref.shape[0]
    chunk = e_ref.shape[1] // (STATE * TILES)
    rate_out[...] = decay_ref[...]
    spread(g_ref[:, DT_RANK : DT_RANK + 2 * STATE].astype(F32), 0, 2 * STATE, bc_ref)
    for j in range(TILES):
        x_ref[pl.ds(j, rows, TILES), :] = mixed_ref[:, lanes_of(j)].astype(F32)
        dt_ref[pl.ds(j, rows, TILES), :] = step_ref[:, lanes_of(j)]
        rate_ref[pl.ds(j, STATE, TILES), :] = decay_ref[:, lanes_of(j)]

    def leave(i, slot):
        size = chunk * STATE * TILES
        at = pl.ds(pl.multiple_of(i * size, size), size)
        return pltpu.make_async_copy(e_ref.at[slot], e_hbm.at[at], sems.at[slot])

    def group(first, slot):
        def one(i, carry):
            states, total = list(carry[:STATE]), carry[STATE]
            t0 = pl.multiple_of(i * UNROLL, UNROLL)
            for r in range(UNROLL):
                t = first + t0 + r
                dt, x = dt_ref[token(t), :], x_ref[token(t), :]
                dx, y = dt * x, gain_ref[...] * x
                total = total + dt
                for n in range(STATE):
                    enter = jnp.broadcast_to(bc_ref[n, pl.ds(t, 1), :], dt.shape)
                    read = jnp.broadcast_to(bc_ref[STATE + n, pl.ds(t, 1), :], dt.shape)
                    states[n] = jnp.exp2(dt * rate_ref[tile(n), :]) * states[n] + dx * enter
                    y = y + states[n] * read
                    e_ref[slot, token((t0 + r) * STATE + n), :] = jnp.exp2(total * rate_ref[tile(n), :]) * read
                y_ref[token(t), :] = y
            return (*states, total)

        return one

    def piece(i, carry):
        slot = lax.rem(i, 2)

        @pl.when(i >= 2)
        def _():
            leave(i - 2, slot).wait()

        carry = lax.fori_loop(0, chunk // UNROLL, group(pl.multiple_of(i * chunk, chunk), slot), carry)
        leave(i, slot).start()
        return carry

    zero = jnp.zeros((TILES, LANES), F32)
    pieces = rows // chunk
    lax.fori_loop(0, pieces, piece, (zero,) * (STATE + 1))
    for i in range(pieces - 2, pieces):
        leave(i, i % 2).wait()


def local(g, dt, rate, mixed, gain):
    rows = mixed.shape[0]
    flat = pltpu.VMEM((rows * TILES, LANES), F32)
    return pl.pallas_call(
        local_kernel,
        out_shape=(
            flat,
            pltpu.HBM((rows * STATE * TILES, LANES), F32),
            pltpu.VMEM(rate.shape, F32),
        ),
        in_specs=[VMEM] * 5,
        out_specs=(VMEM, pl.BlockSpec(memory_space=pltpu.HBM), VMEM),
        scratch_shapes=[
            flat,
            flat,
            pltpu.VMEM((STATE * TILES, LANES), F32),
            pltpu.VMEM((2 * STATE, rows, LANES), F32),
            pltpu.VMEM((2, 32 * STATE * TILES, LANES), F32),
            pltpu.SemaphoreType.DMA((2,)),
        ],
        compiler_params=params(12),
        cost_estimate=cost(60_000_000),
        name="local",
    )(g, dt, rate, mixed, gain)


def unpack_sums(got_ref, count, sum_ref):
    for k in range(count):
        both = got_ref[PACK * (k + 1) - 2 * TILES : PACK * (k + 1), :].astype(F32)
        sum_ref[TILES * k : TILES * (k + 1), :] = both[:TILES] + both[TILES:]


def hand_on(got_ref, sum_ref, rate, k, j, run):
    end = got_ref[PACK * k + STATE * j : PACK * k + STATE * (j + 1), :].astype(F32)
    steps = jnp.broadcast_to(sum_ref[TILES * k + j : TILES * k + j + 1, :], end.shape)
    return jnp.exp2(steps * rate) * run + end


def merge_kernel(got_ref, rate_ref, send_ref, state_ref, before_ref, sum_ref, whole_ref):
    rows, count = send_ref.shape[0] // PACK, got_ref.shape[0] // PACK
    me = lax.axis_index("seq")
    z, x = lax.rem(me, Z), me // Z
    unpack_sums(got_ref, count, sum_ref)
    whole = before = jnp.zeros((TILES, LANES), F32)
    for k in range(count):
        steps = sum_ref[TILES * k : TILES * (k + 1), :]
        whole = whole + steps
        before = before + jnp.where(k < z, steps, 0.0)
    before_ref[...] = before
    whole_ref[...] = whole
    for j in range(TILES):
        rate = rate_ref[:, lanes_of(j)]
        run = kept = jnp.zeros((STATE, LANES), F32)
        for k in range(count):
            kept = jnp.where(k == z, run, kept)
            run = hand_on(got_ref, sum_ref, rate, k, j, run)
        state_ref[STATE * j : STATE * (j + 1), :] = kept
        for d in range(rows):
            send_ref[PACK * d + STATE * j : PACK * d + STATE * (j + 1), :] = jnp.where(d > x, run, 0.0).astype(BF16)
    for d in range(rows):
        send_sums(whole_ref, send_ref, PACK * d + STATE * TILES, d > x)


def merge(got, rate, rows):
    return pl.pallas_call(
        merge_kernel,
        out_shape=(
            jax.ShapeDtypeStruct((rows * PACK, LANES), BF16),
            pltpu.VMEM((STATE * TILES, LANES), F32),
            pltpu.VMEM((TILES, LANES), F32),
        ),
        in_specs=[VMEM, VMEM],
        out_specs=(VMEM,) * 3,
        scratch_shapes=[pltpu.VMEM((Z * TILES, LANES), F32), pltpu.VMEM((TILES, LANES), F32)],
        compiler_params=params(8),
        cost_estimate=cost(200_000_000),
        name="merge",
    )(got, rate)


def finish_kernel(
    got_ref, state_ref, before_ref, rate_ref, y_ref, e_ref, out_hbm, tot_ref, out_ref, sum_ref, in_ref, sems
):
    rows = out_hbm.shape[0]
    count = got_ref.shape[0] // PACK - 1
    unpack_sums(got_ref, count, sum_ref)
    for j in range(TILES):
        rate = rate_ref[:, lanes_of(j)]
        run = jnp.zeros((STATE, LANES), F32)
        for k in range(count):
            run = hand_on(got_ref, sum_ref, rate, k, j, run)
        steps = jnp.broadcast_to(before_ref[j : j + 1, :], run.shape)
        at = slice(STATE * j, STATE * (j + 1))
        in_ref[at, :] = jnp.exp2(steps * rate) * run + state_ref[at, :]
    incoming = [in_ref[pl.ds(n, TILES, STATE), :] for n in range(STATE)]

    def group(i, carry):
        t0 = pl.multiple_of(i * UNROLL, UNROLL)
        for r in range(UNROLL):
            t = t0 + r
            more = [e_ref[token(t * STATE + n), :] * carry[n] for n in range(STATE)]
            while len(more) > 1:
                more = [a + b for a, b in zip(more[::2], more[1::2])]
            tot_ref[token(t), :] = y_ref[token(t), :] + more[0]
        return carry

    pieces = sems.shape[0]
    some = rows // pieces

    def leave(i):
        at = pl.ds(pl.multiple_of(i * some, some), some)
        return pltpu.make_async_copy(out_ref.at[at], out_hbm.at[at], sems.at[i])

    def piece(i, carry):
        lax.fori_loop(i * (some // UNROLL), (i + 1) * (some // UNROLL), group, carry)
        at = pl.ds(pl.multiple_of(i * some, some), some)
        for j in range(TILES):
            rows_j = tot_ref[pl.ds(i * (some * TILES) + j, some, TILES), :]
            out_ref[at, LANES * j : LANES * (j + 1)] = rows_j.astype(BF16)
        leave(i).start()
        return carry

    lax.fori_loop(0, pieces, piece, tuple(incoming))
    for i in range(pieces):
        leave(i).wait()


def finish(got, states, sums, rate, y, e):
    rows = y.shape[0] // TILES
    return pl.pallas_call(
        finish_kernel,
        out_shape=jax.ShapeDtypeStruct((rows, TILES * LANES), BF16),
        in_specs=[VMEM] * 6,
        out_specs=pl.BlockSpec(memory_space=pltpu.HBM),
        scratch_shapes=[
            pltpu.VMEM(y.shape, F32),
            pltpu.VMEM((rows, TILES * LANES), BF16),
            pltpu.VMEM((Z * TILES, LANES), F32),
            pltpu.VMEM((STATE * TILES, LANES), F32),
            pltpu.SemaphoreType.DMA((4,)),
        ],
        compiler_params=params(8),
        name="finish",
    )(got, states, sums, rate, y, e)


def shards(inputs, conv_weight, conv_bias, proj_weight, dt_weight, dt_bias, decay_rate, skip_gain):
    rows, width = inputs.shape
    seq, mp = lax.axis_size("seq"), lax.axis_size("mp")
    x_size, y_size = seq // Z, mp // 2
    on_z = [[Z * x + z for z in range(Z)] for x in range(x_size)]
    on_x = [[Z * x + z for x in range(x_size)] for z in range(Z)]
    on_y = [[2 * y + core for y in range(y_size)] for core in range(2)]
    on_chip = [[2 * y, 2 * y + 1] for y in range(y_size)]

    halo = lax.ppermute(inputs[rows - 8 :], "seq", [(s, s + 1) for s in range(seq - 1)])
    mixed, head, taps_in, bias, weight, dtw, dtb, rate, gain = mix(
        inputs,
        conv_weight,
        conv_bias.reshape(1, width),
        jnp.transpose(proj_weight),
        dt_weight,
        dt_bias.reshape(1, width),
        jnp.transpose(decay_rate),
        skip_gain.reshape(1, width),
    )
    mixed, share, theirs = project(mixed, head, halo, taps_in, bias, weight)
    both = lax.all_gather(theirs, "mp", axis=0, tiled=True, axis_index_groups=on_chip)
    parts = lax.all_to_all(pair(share, both), "mp", 0, 0, tiled=True, axis_index_groups=on_y)
    mine = lax.all_to_all(total(parts), "mp", 0, 0, tiled=True, axis_index_groups=on_y)
    projected = lax.all_gather(mine, "mp", axis=0, tiled=True, axis_index_groups=on_chip)
    dt, ends = state(projected, dtw, dtb, mixed, rate)
    got = lax.all_to_all(ends, "seq", 0, 0, tiled=True, axis_index_groups=on_z)
    y, e, rate = local(projected, dt, rate, mixed, gain)
    ends, states, sums = merge(got, rate, x_size)
    got = lax.all_to_all(ends, "seq", 0, 0, tiled=True, axis_index_groups=on_x)
    return finish(got, states, sums, rate, y, e)


def solution(mesh):
    placed = (
        P("seq", "mp"),
        P(None, "mp"),
        P("mp"),
        P("mp", None),
        P(None, "mp"),
        P("mp"),
        P("mp", None),
        P("mp"),
    )
    return jax.shard_map(
        shards, mesh=mesh, in_specs=placed, out_specs=P("seq", "mp"), check_vma=False
    )
```

```python
import jax
import jax.numpy as jnp
from jax import lax
from jax.experimental import pallas as pl
from jax.experimental.pallas import tpu as pltpu
from jax.sharding import PartitionSpec as P

F32, BF16 = jnp.float32, jnp.bfloat16
STATE = 16
DT_RANK = 512
LANES, TILES = 128, 8
LOG2E = 1.4426950408889634
PACK = STATE * TILES + 2 * TILES
Z = 8
UNROLL = 16
VMEM = pl.BlockSpec(memory_space=pltpu.VMEM)


def params(mib):
    return pltpu.CompilerParams(vmem_limit_bytes=mib << 20)


def cost(flops):
    return pl.CostEstimate(flops=flops, bytes_accessed=flops // 4, transcendentals=flops // 8)


def taps(pad_ref, w_ref, b_ref, first, count):
    pre = b_ref[...] + w_ref[0:1, :] * pad_ref[first + 5 : first + 5 + count, :]
    for k in range(1, 4):
        pre = pre + w_ref[k : k + 1, :] * pad_ref[first + 5 + k : first + 5 + k + count, :]
    return pre / (1.0 + jnp.exp(-pre))


def mix_kernel(
    x_hbm, w_hbm, b_hbm, pw_hbm, dtw_hbm, dtb_hbm, decay_hbm, gain_hbm,
    mixed_ref, head_ref, w_ref, b_ref, pw_ref, dtw_ref, dtb_ref, rate_ref, gain_ref,
    x_ref, pad_ref, decay_ref, row_ref, sems,
):
    rows = x_hbm.shape[0]
    step, parts = 16, 4
    some = rows // parts
    small = [
        pltpu.make_async_copy(source, target, sems.at[i])
        for i, (source, target) in enumerate(((w_hbm, w_ref), (b_hbm, b_ref)))
    ]
    chunks = [
        pltpu.make_async_copy(x_hbm.at[pl.ds(some * i, some)], x_ref.at[pl.ds(some * i, some)], sems.at[2 + i])
        for i in range(parts)
    ]
    later = [
        pltpu.make_async_copy(source, target, sems.at[2 + parts + i])
        for i, (source, target) in enumerate(
            ((decay_hbm, decay_ref), (gain_hbm, row_ref), (pw_hbm, pw_ref), (dtw_hbm, dtw_ref), (dtb_hbm, dtb_ref))
        )
    ]
    for copy in small + chunks + later:
        copy.start()
    pad_ref[0:8, :] = jnp.zeros_like(pad_ref[0:8, :])
    for copy in small:
        copy.wait()
    for i, copy in enumerate(chunks):
        copy.wait()
        for r in range(some * i, some * (i + 1), step):
            pad_ref[8 + r : 8 + r + step, :] = x_ref[r : r + step, :].astype(F32)
            mixed_ref[r : r + step, :] = taps(pad_ref, w_ref, b_ref, r, step).astype(BF16)
    head_ref[...] = pad_ref[8:16, :]
    for copy in later:
        copy.wait()
    for j in range(TILES):
        gain_ref[j : j + 1, :] = row_ref[:, lanes_of(j)]
    rate_ref[...] = decay_ref[...] * -LOG2E


def mix(x, weight, bias, weight_t, dtw, dtb, decay, gain):
    rows, width = x.shape
    return pl.pallas_call(
        mix_kernel,
        out_shape=(
            pltpu.VMEM((rows, width), BF16),
            pltpu.VMEM((8, width), F32),
            pltpu.VMEM(weight.shape, F32),
            pltpu.VMEM(bias.shape, F32),
            pltpu.VMEM(weight_t.shape, BF16),
            pltpu.VMEM(dtw.shape, BF16),
            pltpu.VMEM(dtb.shape, F32),
            pltpu.VMEM(decay.shape, F32),
            pltpu.VMEM((TILES, LANES), F32),
        ),
        in_specs=[pl.BlockSpec(memory_space=pltpu.HBM)] * 8,
        out_specs=(VMEM,) * 9,
        scratch_shapes=[
            pltpu.VMEM((rows, width), BF16),
            pltpu.VMEM((rows + 8, width), F32),
            pltpu.VMEM(decay.shape, F32),
            pltpu.VMEM(gain.shape, F32),
            pltpu.SemaphoreType.DMA((11,)),
        ],
        compiler_params=params(60),
        cost_estimate=cost(20_000_000),
        name="mix",
    )(x, weight, bias, weight_t, dtw, dtb, decay, gain)


def project_kernel(
    mixed_in, head_ref, halo_ref, w_ref, b_ref, pw_ref, mixed_ref, share_ref, theirs_ref, pad_ref
):
    pad_ref[0:8, :] = halo_ref[...].astype(F32)
    pad_ref[8:16, :] = head_ref[...]
    top = taps(pad_ref, w_ref, b_ref, 0, 8)
    mixed_ref[16:, :] = mixed_in[16:, :]
    mixed_ref[0:16, :] = jnp.concatenate([top, mixed_in[0:16, :].astype(F32)[8:16]], axis=0).astype(BF16)
    share_ref[...] = lax.dot_general(
        mixed_ref[...], pw_ref[...], (((1,), (1,)), ((), ())), preferred_element_type=F32
    ).astype(BF16)
    half = theirs_ref.shape[0]
    core = lax.rem(lax.axis_index("mp"), 2)
    theirs_ref[...] = share_ref[pl.ds(pl.multiple_of((1 - core) * half, half), half), :]


def project(mixed, head, halo, weight, bias, weight_t):
    rows, width = mixed.shape
    columns = weight_t.shape[0]
    return pl.pallas_call(
        project_kernel,
        out_shape=(
            pltpu.VMEM((rows, width), BF16),
            pltpu.VMEM((rows, columns), BF16),
            pltpu.VMEM((rows // 2, columns), BF16),
        ),
        in_specs=[VMEM] * 6,
        out_specs=(VMEM,) * 3,
        scratch_shapes=[pltpu.VMEM((16, width), F32)],
        compiler_params=params(8),
        name="project",
    )(mixed, head, halo, weight, bias, weight_t)


def pair_kernel(share_ref, got_ref, out_ref):
    half = out_ref.shape[0]
    core = lax.rem(lax.axis_index("mp"), 2)
    ours = share_ref[pl.ds(pl.multiple_of(core * half, half), half), :]
    theirs = got_ref[pl.ds(pl.multiple_of((1 - core) * half, half), half), :]
    out_ref[...] = (ours.astype(F32) + theirs.astype(F32)).astype(BF16)


def pair(share, got):
    return pl.pallas_call(
        pair_kernel,
        out_shape=jax.ShapeDtypeStruct((share.shape[0] // 2, share.shape[1]), BF16),
        in_specs=[VMEM] * 2,
        out_specs=VMEM,
        compiler_params=params(8),
        name="pair",
    )(share, got)


def total_kernel(parts_ref, out_ref):
    rows = 16
    total = parts_ref[0:rows, :].astype(F32)
    for k in range(1, parts_ref.shape[0] // rows):
        total = total + parts_ref[rows * k : rows * (k + 1), :].astype(F32)
    for k in range(out_ref.shape[0] // rows):
        out_ref[rows * k : rows * (k + 1), :] = total.astype(BF16)


def total(parts):
    return pl.pallas_call(
        total_kernel,
        out_shape=jax.ShapeDtypeStruct(parts.shape, BF16),
        in_specs=[VMEM],
        out_specs=VMEM,
        compiler_params=params(8),
        name="total",
    )(parts)


def spread(columns, first, count, out_ref):
    for n in range(count):
        out_ref[n] = jnp.broadcast_to(
            columns[:, first + n : first + n + 1], (columns.shape[0], LANES)
        )


def lanes_of(j):
    return slice(LANES * j, LANES * (j + 1))


def tile(n):
    return slice(TILES * n, TILES * (n + 1))


def token(t):
    return pl.ds(pl.multiple_of(t * TILES, TILES), TILES)


def send_sums(row_ref, send_ref, at, keep=None):
    value = row_ref[...]
    high = value.astype(BF16).astype(F32)
    both = jnp.concatenate([high, value - high], axis=0)
    if keep is not None:
        both = jnp.where(keep, both, 0.0)
    send_ref[at : at + 2 * TILES, :] = both.astype(BF16)


def state_kernel(
    g_ref, dtw_ref, dtb_ref, mixed_ref, rate_ref, dt_hbm, send_ref, dt_ref, enter_ref, sum_ref, sems
):
    rows, width = mixed_ref.shape
    low = g_ref[:, 0:DT_RANK]
    enter = jnp.transpose(g_ref[:, DT_RANK : DT_RANK + 2 * STATE].astype(F32))[:STATE]
    row = lax.broadcasted_iota(jnp.int32, enter.shape, 0)
    for n in range(STATE):
        enter_ref[STATE * n : STATE * (n + 1), :] = jnp.where(row == n, enter, 0.0).astype(BF16)
    here = lax.broadcasted_iota(jnp.int32, (rows, rows), 0)
    there = lax.broadcasted_iota(jnp.int32, (rows, rows), 1)
    later = (there > here).astype(F32).astype(BF16)
    copies = []
    for c in range(0, width, 256):
        at = slice(c, c + 256)
        pre = jnp.dot(low, dtw_ref[:, at], preferred_element_type=F32) + dtb_ref[:, at]
        small = jnp.exp(-jnp.abs(pre))
        log1p = jnp.where(small < 1e-3, small - 0.5 * small * small, jnp.log(1.0 + small))
        dt = jnp.maximum(pre, 0.0) + log1p
        dt_ref[:, at] = dt
        whole = jnp.sum(dt, axis=0, keepdims=True)
        for h in range(2):
            sum_ref[c // LANES + h : c // LANES + h + 1, :] = whole[:, lanes_of(h)]
    copies.append(pltpu.make_async_copy(dt_ref, dt_hbm, sems.at[0]))
    copies[-1].start()
    for c in range(0, width, 256):
        at = slice(c, c + 256)
        dt = dt_ref[:, at]
        dx = dt * mixed_ref[:, at].astype(F32)
        rem = jnp.dot(later, dt.astype(BF16), preferred_element_type=F32)
        ends = jnp.zeros((STATE, 256), F32)
        for n in range(STATE):
            part = (jnp.exp2(rem * rate_ref[n : n + 1, at]) * dx).astype(BF16)
            ends = ends + jnp.dot(enter_ref[STATE * n : STATE * (n + 1), :], part, preferred_element_type=F32)
        for h in range(2):
            j = c // LANES + h
            for k in range(Z):
                send_ref[PACK * k + STATE * j : PACK * k + STATE * (j + 1), :] = ends[:, lanes_of(h)].astype(BF16)
    for k in range(Z):
        send_sums(sum_ref, send_ref, PACK * k + STATE * TILES)
    for copy in copies:
        copy.wait()


def state(g, dtw, dtb, mixed, rate):
    rows, width = mixed.shape
    return pl.pallas_call(
        state_kernel,
        out_shape=(
            pltpu.HBM((rows, width), F32),
            pltpu.VMEM((Z * PACK, LANES), BF16),
        ),
        in_specs=[VMEM] * 5,
        out_specs=(pl.BlockSpec(memory_space=pltpu.HBM), VMEM),
        scratch_shapes=[
            pltpu.VMEM((rows, width), F32),
            pltpu.VMEM((STATE * STATE, rows), BF16),
            pltpu.VMEM((TILES, LANES), F32),
            pltpu.SemaphoreType.DMA((1,)),
        ],
        compiler_params=params(12),
        name="state",
    )(g, dtw, dtb, mixed, rate)


def local_kernel(
    g_ref, step_ref, decay_ref, mixed_ref, gain_ref, y_ref, e_hbm, rate_out, x_ref, dt_ref, rate_ref, bc_ref, e_ref, sems
):
    rows = mixed_ref.shape[0]
    chunk = e_ref.shape[1] // (STATE * TILES)
    rate_out[...] = decay_ref[...]
    spread(g_ref[:, DT_RANK : DT_RANK + 2 * STATE].astype(F32), 0, 2 * STATE, bc_ref)
    for j in range(TILES):
        x_ref[pl.ds(j, rows, TILES), :] = mixed_ref[:, lanes_of(j)].astype(F32)
        dt_ref[pl.ds(j, rows, TILES), :] = step_ref[:, lanes_of(j)]
        rate_ref[pl.ds(j, STATE, TILES), :] = decay_ref[:, lanes_of(j)]

    def leave(i, slot):
        size = chunk * STATE * TILES
        at = pl.ds(pl.multiple_of(i * size, size), size)
        return pltpu.make_async_copy(e_ref.at[slot], e_hbm.at[at], sems.at[slot])

    def group(first, slot):
        def one(i, carry):
            states, total = list(carry[:STATE]), carry[STATE]
            t0 = pl.multiple_of(i * UNROLL, UNROLL)
            for r in range(UNROLL):
                t = first + t0 + r
                dt, x = dt_ref[token(t), :], x_ref[token(t), :]
                dx, y = dt * x, gain_ref[...] * x
                total = total + dt
                for n in range(STATE):
                    enter = jnp.broadcast_to(bc_ref[n, pl.ds(t, 1), :], dt.shape)
                    read = jnp.broadcast_to(bc_ref[STATE + n, pl.ds(t, 1), :], dt.shape)
                    states[n] = jnp.exp2(dt * rate_ref[tile(n), :]) * states[n] + dx * enter
                    y = y + states[n] * read
                    e_ref[slot, token((t0 + r) * STATE + n), :] = jnp.exp2(total * rate_ref[tile(n), :]) * read
                y_ref[token(t), :] = y
            return (*states, total)

        return one

    def piece(i, carry):
        slot = lax.rem(i, 2)

        @pl.when(i >= 2)
        def _():
            leave(i - 2, slot).wait()

        carry = lax.fori_loop(0, chunk // UNROLL, group(pl.multiple_of(i * chunk, chunk), slot), carry)
        leave(i, slot).start()
        return carry

    zero = jnp.zeros((TILES, LANES), F32)
    pieces = rows // chunk
    lax.fori_loop(0, pieces, piece, (zero,) * (STATE + 1))
    for i in range(pieces - 2, pieces):
        leave(i, i % 2).wait()


def local(g, dt, rate, mixed, gain):
    rows = mixed.shape[0]
    flat = pltpu.VMEM((rows * TILES, LANES), F32)
    return pl.pallas_call(
        local_kernel,
        out_shape=(
            flat,
            pltpu.HBM((rows * STATE * TILES, LANES), F32),
            pltpu.VMEM(rate.shape, F32),
        ),
        in_specs=[VMEM] * 5,
        out_specs=(VMEM, pl.BlockSpec(memory_space=pltpu.HBM), VMEM),
        scratch_shapes=[
            flat,
            flat,
            pltpu.VMEM((STATE * TILES, LANES), F32),
            pltpu.VMEM((2 * STATE, rows, LANES), F32),
            pltpu.VMEM((2, 32 * STATE * TILES, LANES), F32),
            pltpu.SemaphoreType.DMA((2,)),
        ],
        compiler_params=params(12),
        cost_estimate=cost(60_000_000),
        name="local",
    )(g, dt, rate, mixed, gain)


def unpack_sums(got_ref, count, sum_ref):
    for k in range(count):
        both = got_ref[PACK * (k + 1) - 2 * TILES : PACK * (k + 1), :].astype(F32)
        sum_ref[TILES * k : TILES * (k + 1), :] = both[:TILES] + both[TILES:]


def hand_on(got_ref, sum_ref, rate, k, j, run):
    end = got_ref[PACK * k + STATE * j : PACK * k + STATE * (j + 1), :].astype(F32)
    steps = jnp.broadcast_to(sum_ref[TILES * k + j : TILES * k + j + 1, :], end.shape)
    return jnp.exp2(steps * rate) * run + end


def merge_kernel(got_ref, rate_ref, send_ref, state_ref, before_ref, sum_ref, whole_ref):
    rows, count = send_ref.shape[0] // PACK, got_ref.shape[0] // PACK
    me = lax.axis_index("seq")
    z, x = lax.rem(me, Z), me // Z
    unpack_sums(got_ref, count, sum_ref)
    whole = before = jnp.zeros((TILES, LANES), F32)
    for k in range(count):
        steps = sum_ref[TILES * k : TILES * (k + 1), :]
        whole = whole + steps
        before = before + jnp.where(k < z, steps, 0.0)
    before_ref[...] = before
    whole_ref[...] = whole
    for j in range(TILES):
        rate = rate_ref[:, lanes_of(j)]
        run = kept = jnp.zeros((STATE, LANES), F32)
        for k in range(count):
            kept = jnp.where(k == z, run, kept)
            run = hand_on(got_ref, sum_ref, rate, k, j, run)
        state_ref[STATE * j : STATE * (j + 1), :] = kept
        for d in range(rows):
            send_ref[PACK * d + STATE * j : PACK * d + STATE * (j + 1), :] = jnp.where(d > x, run, 0.0).astype(BF16)
    for d in range(rows):
        send_sums(whole_ref, send_ref, PACK * d + STATE * TILES, d > x)


def merge(got, rate, rows):
    return pl.pallas_call(
        merge_kernel,
        out_shape=(
            jax.ShapeDtypeStruct((rows * PACK, LANES), BF16),
            pltpu.VMEM((STATE * TILES, LANES), F32),
            pltpu.VMEM((TILES, LANES), F32),
        ),
        in_specs=[VMEM, VMEM],
        out_specs=(VMEM,) * 3,
        scratch_shapes=[pltpu.VMEM((Z * TILES, LANES), F32), pltpu.VMEM((TILES, LANES), F32)],
        compiler_params=params(8),
        cost_estimate=cost(200_000_000),
        name="merge",
    )(got, rate)


def finish_kernel(
    got_ref, state_ref, before_ref, rate_ref, y_ref, e_ref, out_hbm, tot_ref, out_ref, sum_ref, in_ref, sems
):
    rows = out_hbm.shape[0]
    count = got_ref.shape[0] // PACK - 1
    unpack_sums(got_ref, count, sum_ref)
    for j in range(TILES):
        rate = rate_ref[:, lanes_of(j)]
        run = jnp.zeros((STATE, LANES), F32)
        for k in range(count):
            run = hand_on(got_ref, sum_ref, rate, k, j, run)
        steps = jnp.broadcast_to(before_ref[j : j + 1, :], run.shape)
        at = slice(STATE * j, STATE * (j + 1))
        in_ref[at, :] = jnp.exp2(steps * rate) * run + state_ref[at, :]
    incoming = [in_ref[pl.ds(n, TILES, STATE), :] for n in range(STATE)]

    def group(i, carry):
        t0 = pl.multiple_of(i * UNROLL, UNROLL)
        for r in range(UNROLL):
            t = t0 + r
            more = [e_ref[token(t * STATE + n), :] * carry[n] for n in range(STATE)]
            while len(more) > 1:
                more = [a + b for a, b in zip(more[::2], more[1::2])]
            tot_ref[token(t), :] = y_ref[token(t), :] + more[0]
        return carry

    pieces = sems.shape[0]
    some = rows // pieces

    def leave(i):
        at = pl.ds(pl.multiple_of(i * some, some), some)
        return pltpu.make_async_copy(out_ref.at[at], out_hbm.at[at], sems.at[i])

    def piece(i, carry):
        lax.fori_loop(i * (some // UNROLL), (i + 1) * (some // UNROLL), group, carry)
        at = pl.ds(pl.multiple_of(i * some, some), some)
        for j in range(TILES):
            rows_j = tot_ref[pl.ds(i * (some * TILES) + j, some, TILES), :]
            out_ref[at, LANES * j : LANES * (j + 1)] = rows_j.astype(BF16)
        leave(i).start()
        return carry

    lax.fori_loop(0, pieces, piece, tuple(incoming))
    for i in range(pieces):
        leave(i).wait()


def finish(got, states, sums, rate, y, e):
    rows = y.shape[0] // TILES
    return pl.pallas_call(
        finish_kernel,
        out_shape=jax.ShapeDtypeStruct((rows, TILES * LANES), BF16),
        in_specs=[VMEM] * 6,
        out_specs=pl.BlockSpec(memory_space=pltpu.HBM),
        scratch_shapes=[
            pltpu.VMEM(y.shape, F32),
            pltpu.VMEM((rows, TILES * LANES), BF16),
            pltpu.VMEM((Z * TILES, LANES), F32),
            pltpu.VMEM((STATE * TILES, LANES), F32),
            pltpu.SemaphoreType.DMA((4,)),
        ],
        compiler_params=params(8),
        name="finish",
    )(got, states, sums, rate, y, e)


def shards(inputs, conv_weight, conv_bias, proj_weight, dt_weight, dt_bias, decay_rate, skip_gain):
    rows, width = inputs.shape
    seq, mp = lax.axis_size("seq"), lax.axis_size("mp")
    x_size, y_size = seq // Z, mp // 2
    on_z = [[Z * x + z for z in range(Z)] for x in range(x_size)]
    on_x = [[Z * x + z for x in range(x_size)] for z in range(Z)]
    on_y = [[2 * y + core for y in range(y_size)] for core in range(2)]
    on_chip = [[2 * y, 2 * y + 1] for y in range(y_size)]

    halo = lax.ppermute(inputs[rows - 8 :], "seq", [(s, s + 1) for s in range(seq - 1)])
    mixed, head, taps_in, bias, weight, dtw, dtb, rate, gain = mix(
        inputs,
        conv_weight,
        conv_bias.reshape(1, width),
        jnp.transpose(proj_weight),
        dt_weight,
        dt_bias.reshape(1, width),
        jnp.transpose(decay_rate),
        skip_gain.reshape(1, width),
    )
    mixed, share, theirs = project(mixed, head, halo, taps_in, bias, weight)
    both = lax.all_gather(theirs, "mp", axis=0, tiled=True, axis_index_groups=on_chip)
    parts = lax.all_to_all(pair(share, both), "mp", 0, 0, tiled=True, axis_index_groups=on_y)
    mine = lax.all_to_all(total(parts), "mp", 0, 0, tiled=True, axis_index_groups=on_y)
    projected = lax.all_gather(mine, "mp", axis=0, tiled=True, axis_index_groups=on_chip)
    dt, ends = state(projected, dtw, dtb, mixed, rate)
    got = lax.all_to_all(ends, "seq", 0, 0, tiled=True, axis_index_groups=on_z)
    y, e, rate = local(projected, dt, rate, mixed, gain)
    ends, states, sums = merge(got, rate, x_size)
    got = lax.all_to_all(ends, "seq", 0, 0, tiled=True, axis_index_groups=on_x)
    return finish(got, states, sums, rate, y, e)


def solution(mesh):
    placed = (
        P("seq", "mp"),
        P(None, "mp"),
        P("mp"),
        P("mp", None),
        P(None, "mp"),
        P("mp"),
        P("mp", None),
        P("mp"),
    )
    return jax.shard_map(
        shards, mesh=mesh, in_specs=placed, out_specs=P("seq", "mp"), check_vma=False
    )
```
